32 devices in a mesh: row: 8 (over z, core), col: 4 (over y, x).
Axes of the slice: x: 2, y: 2, z: 4, core: 2. Of those that a mesh axis runs over, the one named last changes fastest.
Arguments:
- stress: float32 [256, 4096], P('col', 'row'), may hold values from -2.5 to 2.5
- state: float32 [256, 2048], P('col', 'row'), may hold values from 0 to 1
- load_rate: int32 [256, 4096], P('col', 'row'), may hold values from 0 to 2047
- a_param: float32 [2048], P('row'), may hold values from 1 to 2
- b_param: float32 [2048], P('row'), may hold values from 0.25 to 1
- near_band: bfloat16 [4096, 768], P('row'), may hold values from -0.21875 to 0.21875
- u_far: bfloat16 [16, 16, 32, 256], P('row', 'col'), may hold values from -0.375 to 0.375
- v_far: bfloat16 [16, 16, 32, 256], P('row', 'col'), may hold values from -0.375 to 0.375
- ranks: int32 [16, 16], P('row', 'col'), may hold values from 1 to 32, as said below
Outputs:
- new_stress: float32 [256, 4096], P('col', 'row')
- new_state: float32 [256, 2048], P('col', 'row')
The draws below stay inside these ranges and needn't reach their ends.
Inputs may be any that keep to these rules, and one draw needn't show every extreme that they name: ranks of blocks with |I - J| <= 1 are not used; blocks with |I - J| = 2 have rank 32.
All inputs are finite; a program needn't handle non-finite values.
Results may differ from the reference program's by a relative error of at most 0.0021.
Values may be sent and summed in bfloat16 or wider, within the bound.
A program may use at most 64 MiB of HBM per device.

```python
import math
import jax
import jax.numpy as jnp
from jax import lax

B = 128
RK = 32
MEMBERS = 256
NB = 16
NE = 2048
NDOF = 4096


def draw_ranks(key, part):
    drawn = jax.random.randint(key, (NB, NB), 1, RK + 1)
    blocks = jnp.arange(NB)
    spacing = jnp.abs(blocks[:, None] - blocks[None, :])
    return jnp.where(spacing == 2, RK, drawn).astype(jnp.int32)


def set_ends(values, key, least, largest):
    place = [jax.random.randint(jax.random.fold_in(key, axis), (), 0, length) for axis, length in enumerate(values.shape)]
    main_axis = values.shape.index(max(values.shape))
    next_to = place[:main_axis] + [(place[main_axis] + 1) % values.shape[main_axis]] + place[main_axis + 1:]
    return values.at[tuple(place)].set(least).at[tuple(next_to)].set(largest)


def block_levels(stream_key, shape, split, smallest, largest):
    def one(axis_at, shards_of):
        draws = jax.random.uniform(jax.random.fold_in(jax.random.fold_in(stream_key, 6), axis_at), (shards_of,), jnp.float32, smallest / len(split), largest / len(split))
        return jnp.repeat(jnp.exp(draws), shape[axis_at] // shards_of).reshape((-1,) + (1,) * (len(shape) - axis_at - 1))

    factor_of = one(*split[0])
    for cut in split[1:]:
        factor_of = factor_of * one(*cut)
    return factor_of


def normal_values(rng, dims, deviation, bound, cuts=(), kind=jnp.bfloat16):
    result = jax.random.normal(rng, dims, jnp.float32) * deviation
    if len(cuts) > 0:
        result = block_levels(rng, dims, cuts, -0.22, 0.18) * result
    return jnp.clip(result, min=-bound, max=bound).astype(kind)


def setup_inputs(seed: int = 0) -> dict:
    key_of = jax.random.split(jax.random.key(seed), 10)
    stress = normal_values(key_of[0], (MEMBERS, NDOF), 0.3, 2.5, ((0, 4), (1, 8)), jnp.float32)
    state = jnp.clip(1.0 * jax.random.uniform(key_of[1], (MEMBERS, NE), jnp.float32) ** block_levels(key_of[1], (MEMBERS, NE), ((0, 4), (1, 8)), -0.2, 0.2), 0.0, 1.0)
    load_rate = set_ends(jax.random.randint(key_of[2], (MEMBERS, NDOF), 0, 2048), jax.random.fold_in(key_of[2], 1), 0, 2047).astype(jnp.int32)
    a_param = jnp.clip(jnp.exp(math.log(2.0) - 0.6931472 * jax.random.uniform(key_of[3], (NE,), jnp.float32) ** block_levels(key_of[3], (NE,), ((0, 8),), -0.2, 0.2)), 1.0, 2.0)
    b_param = jnp.clip(jnp.exp(math.log(1.0) - 1.3862944 * jax.random.uniform(key_of[4], (NE,), jnp.float32) ** block_levels(key_of[4], (NE,), ((0, 8),), -0.2, 0.2)), 0.25, 1.0)
    near_band = normal_values(key_of[5], (NDOF, 6 * B), (6 * B) ** -0.5, 0.21875, ((0, 8),))
    u_far = normal_values(key_of[6], (NB, NB, RK, 2 * B), (RK * NB // 2) ** -0.5, 0.375, ((0, 8), (1, 4)))
    v_far = normal_values(key_of[7], (NB, NB, RK, 2 * B), (2 * B) ** -0.5, 0.375, ((0, 8), (1, 4)))
    ranks = draw_ranks(jax.random.fold_in(key_of[9], 71), 0)
    return {"stress": stress, "state": state, "load_rate": load_rate, "a_param": a_param, "b_param": b_param, "near_band": near_band, "u_far": u_far, "v_far": v_far, "ranks": ranks}


HSTEP = 0.2
RATE_UNIT = 1.0 / 1024.0

def rates_and_drift(stress_now, state_now, plate_rate, a_param, b_param):
    members = stress_now.shape[0]
    block_count = a_param.shape[0] // B
    stress_view = stress_now.reshape(members, block_count, 2, B)
    state_view = state_now.reshape(members, block_count, 1, B)
    direct_view = a_param.reshape(1, block_count, 1, B)
    evolve_view = b_param.reshape(1, block_count, B)
    slip_rate = 2.0 * jnp.exp(-state_view) * jnp.sinh(stress_view / direct_view)
    slip_speed = jnp.sqrt(lax.optimization_barrier(jnp.sum(slip_rate * slip_rate, axis=2)))
    drift = evolve_view * (jnp.exp(-state_view[:, :, 0]) - slip_speed)
    excess = (slip_rate - plate_rate.reshape(members, block_count, 2, B)).astype(jnp.bfloat16)
    return (excess.reshape(members, -1), drift.reshape(members, -1))

def reference(stress, state, load_rate, a_param, b_param, near_band, u_far, v_far, ranks):
    plate_rate = load_rate.astype(jnp.float32) * RATE_UNIT
    block_dofs = 2 * B
    slots = jnp.arange(RK, dtype=jnp.int32)
    blocks = jnp.arange(NB, dtype=jnp.int32)

    def tendency(stress_now, state_now):
        excess, drift = rates_and_drift(stress_now, state_now, plate_rate, a_param, b_param)
        grid = excess.reshape(MEMBERS, NB, block_dofs)
        grid_wide = grid.astype(jnp.float32)
        padded = jnp.pad(grid, ((0, 0), (1, 1), (0, 0)))

        def one_row(index):
            v_rows = v_far[index].astype(jnp.float32)
            u_rows = u_far[index].astype(jnp.float32)
            weights = jnp.einsum('mjd,jrd->jmr', grid_wide, v_rows)
            active = (slots[None, :] < ranks[index][:, None]) & (jnp.abs(blocks - index) >= 2)[:, None]
            weights = jnp.where(active[:, None, :], weights, 0.0)
            weights = lax.optimization_barrier(weights.astype(jnp.bfloat16)).astype(jnp.float32)
            distant = jnp.einsum('jmr,jrd->md', weights, u_rows)
            segment = lax.dynamic_slice_in_dim(padded, index, 3, 1).reshape(MEMBERS, 3 * block_dofs)
            local_band = lax.dynamic_slice_in_dim(near_band, index * block_dofs, block_dofs, 0)
            nearby = jnp.dot(segment, local_band.T, preferred_element_type=jnp.float32)
            return distant + nearby
        rows_out = lax.map(one_row, jnp.arange(NB, dtype=jnp.int32))
        totals = jnp.transpose(rows_out, (1, 0, 2)).reshape(MEMBERS, NDOF)
        return (-totals, drift)
    rate_one, drift_one = tendency(stress, state)
    stress_one = stress + HSTEP * rate_one
    state_one = state + HSTEP * drift_one
    rate_two, drift_two = tendency(stress_one, state_one)
    stress_two = 0.75 * stress + 0.25 * (stress_one + HSTEP * rate_two)
    state_two = 0.75 * state + 0.25 * (state_one + HSTEP * drift_two)
    rate_three, drift_three = tendency(stress_two, state_two)
    new_stress = stress / 3.0 + 2.0 / 3.0 * (stress_two + HSTEP * rate_three)
    new_state = state / 3.0 + 2.0 / 3.0 * (state_two + HSTEP * drift_three)
    return (new_stress, new_state)
```

```python
import functools

import jax
import jax.numpy as jnp
from jax import lax
from jax.experimental import pallas as pl
from jax.experimental.pallas import tpu as pltpu
from jax.sharding import PartitionSpec as P

B = 128
HSTEP = 0.2
RATE_UNIT = 1.0 / 1024.0
MESH = pl.DeviceIdType.MESH


def partner(index, step, count):
    assert count & (count - 1) == 0
    bit = 1
    while bit <= step:
        if step & bit:
            index = index + bit - 2 * bit * ((index // bit) % 2)
        bit *= 2
    return index


def dot_t(left, right):
    return lax.dot_general(left, right, (((1,), (1,)), ((), ())), preferred_element_type=jnp.float32)


def kernel(
    rows,
    cols,
    stress_in,
    state_in,
    load_in,
    a_in,
    b_in,
    band_in,
    u_in,
    v_in,
    ranks,
    stress_out,
    state_out,
    stress0,
    state0,
    load,
    band,
    u_all,
    v_all,
    grid,
    load_sem,
    w_send,
    w_recv,
    g_send,
    g_recv,
    f_send,
    f_recv,
):
    row = lax.axis_index("row")
    col = lax.axis_index("col")
    chips = rows // 2
    chip = row // 2
    core = row % 2
    peer = 2 * chip + 1 - core
    _, block_rows, block_cols, slots, dofs = u_all.shape
    members = stress0.shape[0]

    barrier = pltpu.get_barrier_semaphore()
    others = [(row, partner(col, t, cols)) for t in range(1, cols)]
    others += [(2 * partner(chip, t, chips) + core, col) for t in range(1, chips)]
    others += [(peer, col)]
    for other in others:
        pl.semaphore_signal(barrier, inc=1, device_id=other, device_id_type=MESH)

    loads = [
        pltpu.make_async_copy(source, target, load_sem.at[n])
        for n, (source, target) in enumerate(
            [
                (u_in, u_all.at[col]),
                (stress_in, stress0),
                (state_in, state0),
                (load_in, load),
                (v_in, v_all.at[col]),
                (band_in, band),
            ]
        )
    ]
    for copy in loads:
        copy.start()

    loads[0].wait()
    slot = lax.broadcasted_iota(jnp.int32, (slots, dofs), 0)
    for i in range(block_rows):
        for j in range(block_cols):
            spacing = jnp.abs(row * block_rows + i - col * block_cols - j)
            limit = jnp.where(spacing >= 2, ranks[i, j], 0)
            factors = u_all[col, i, j].astype(jnp.float32)
            u_all[col, i, j] = jnp.where(slot < limit, factors, 0.0).astype(jnp.bfloat16)

    pl.semaphore_wait(barrier, len(others))

    def send(source, target, send_sem, recv_sem, device):
        copy = pltpu.make_async_remote_copy(
            src_ref=source,
            dst_ref=target,
            send_sem=send_sem,
            recv_sem=recv_sem,
            device_id=device,
            device_id_type=MESH,
        )
        copy.start()
        return copy

    col_steps = list(range(cols - 1, 0, -1))
    sent = []
    v_copies = {}
    for t in col_steps:
        v_copies[t] = send(
            v_in, v_all.at[col], w_send.at[0, t], w_recv.at[0, t], (row, partner(col, t, cols))
        )
    u_copies = {}

    def send_u():
        for t in col_steps:
            u_copies[t] = send(
                u_all.at[col], u_all.at[col], w_send.at[1, t], w_recv.at[1, t], (row, partner(col, t, cols))
            )

    def weights(s, j):
        parts = []
        per_row = block_cols // 2
        for n in range(block_cols):
            excess = grid[s, 2 * j + n // per_row, :, (n % per_row) * dofs : (n % per_row + 1) * dofs]
            factors = v_all[j, :, n].reshape(block_rows * slots, dofs)
            parts.append(dot_t(excess, factors).astype(jnp.bfloat16))
        return [
            jnp.concatenate([part[:, i * slots : (i + 1) * slots] for part in parts], axis=1)
            for i in range(block_rows)
        ]

    def far(j, weight):
        return [
            jnp.dot(
                weight[i], u_all[j, i].reshape(block_cols * slots, dofs), preferred_element_type=jnp.float32
            )
            for i in range(block_rows)
        ]

    def band_tile(i, n):
        return band[i * dofs : (i + 1) * dofs, n * dofs : (n + 1) * dofs]

    def section(s, stress_now, state_now):
        drift = []
        for i in range(block_rows):
            lanes = slice(i * B, (i + 1) * B)
            theta = state_now[:, lanes]
            direct = a_in[lanes].reshape(1, B)
            squares = None
            for d in range(2):
                dof = slice((2 * i + d) * B, (2 * i + d + 1) * B)
                scaled = stress_now[:, dof] / direct
                rate = jnp.exp(scaled - theta) - jnp.exp(-scaled - theta)
                plate = load[:, dof].astype(jnp.float32) * RATE_UNIT
                grid[s, row, :, dof] = (rate - plate).astype(jnp.bfloat16)
                squares = rate * rate if squares is None else squares + rate * rate
            drift.append((theta, squares, b_in[lanes].reshape(1, B)))
        mine = grid.at[s, row]
        order = list(range(2, chips)) + [1] if chips > 1 else []
        g_copies = {}
        f_copies = {0: send(mine, mine, f_send.at[s, 0], f_recv.at[s, 0], (peer, col))}
        for t in order:
            g_copies[t] = send(
                mine, mine, g_send.at[s, t], g_recv.at[s, t], (2 * partner(chip, t, chips) + core, col)
            )
        if s == 0:
            send_u()
            loads[4].wait()
            loads[5].wait()
        drift = jnp.concatenate(
            [evolve * (jnp.exp(-theta) - jnp.sqrt(squares)) for theta, squares, evolve in drift], axis=1
        )

        total = [None] * block_rows
        for i in range(block_rows):
            for n in range(max(i - 1, 0), min(i + 2, block_rows)):
                term = dot_t(grid[s, row, :, n * dofs : (n + 1) * dofs], band_tile(i, n - i + 1))
                total[i] = term if total[i] is None else total[i] + term

        def add(terms):
            for i in range(block_rows):
                total[i] = total[i] + terms[i]

        def relay(t):
            g_copies[t].wait_recv()
            got = grid.at[s, 2 * partner(chip, t, chips) + core]
            f_copies[t] = send(got, got, f_send.at[s, t], f_recv.at[s, t], (peer, col))

        f_copies[0].wait_recv()
        if s == 0:
            for t in range(1, chips):
                relay(t)
            for t in range(1, chips):
                f_copies[t].wait_recv()
            ready = [(col, weights(s, col))]
            for t in range(1, cols):
                v_copies[t].wait_recv()
                j = partner(col, t, cols)
                ready.append((j, weights(s, j)))
            for t, (j, weight) in enumerate(ready):
                if t > 0:
                    u_copies[t].wait_recv()
                add(far(j, weight))
        else:
            for t in range(1, chips):
                relay(t)
                if t > 1:
                    f_copies[t - 1].wait_recv()
                j = partner(chip, t - 1, chips)
                add(far(j, weights(s, j)))
            if chips > 1:
                f_copies[chips - 1].wait_recv()
            j = partner(chip, chips - 1, chips)
            add(far(j, weights(s, j)))

        left = grid[s, (row + rows - 1) % rows, :, (block_rows - 1) * dofs :]
        right = grid[s, (row + 1) % rows, :, :dofs]
        left_term = dot_t(left, band_tile(0, 0))
        right_term = dot_t(right, band_tile(block_rows - 1, 2))
        total[0] = total[0] + jnp.where(row > 0, left_term, 0.0)
        total[-1] = total[-1] + jnp.where(row < rows - 1, right_term, 0.0)
        sent.extend(g_copies.values())
        sent.extend(f_copies.values())
        return -jnp.concatenate(total, axis=1), drift

    for copy in loads[1:4]:
        copy.wait()
    rate, drift = section(0, stress0[...], state0[...])
    stress_out[...] = stress0[...] + HSTEP * rate
    state_out[...] = state0[...] + HSTEP * drift
    rate, drift = section(1, stress_out[...], state_out[...])
    stress_out[...] = 0.75 * stress0[...] + 0.25 * (stress_out[...] + HSTEP * rate)
    state_out[...] = 0.75 * state0[...] + 0.25 * (state_out[...] + HSTEP * drift)
    rate, drift = section(2, stress_out[...], state_out[...])
    stress_out[...] = stress0[...] / 3.0 + 2.0 / 3.0 * (stress_out[...] + HSTEP * rate)
    state_out[...] = state0[...] / 3.0 + 2.0 / 3.0 * (state_out[...] + HSTEP * drift)
    sent.extend(v_copies.values())
    sent.extend(u_copies.values())
    for copy in sent:
        copy.wait_send()


def local(stress, state, load_rate, a_param, b_param, near_band, u_far, v_far, ranks):
    rows = lax.axis_size("row")
    cols = lax.axis_size("col")
    members, own = stress.shape
    chips = rows // 2
    hbm = pl.BlockSpec(memory_space=pl.ANY)
    vmem = pl.BlockSpec(memory_space=pltpu.VMEM)
    smem = pl.BlockSpec(memory_space=pltpu.SMEM)
    dma = pltpu.SemaphoreType.DMA
    return pl.pallas_call(
        functools.partial(kernel, rows, cols),
        out_shape=(
            jax.ShapeDtypeStruct(stress.shape, jnp.float32),
            jax.ShapeDtypeStruct(state.shape, jnp.float32),
        ),
        in_specs=[hbm, hbm, hbm, vmem, vmem, hbm, hbm, hbm, smem],
        out_specs=(vmem, vmem),
        scratch_shapes=[
            pltpu.VMEM(stress.shape, jnp.float32),
            pltpu.VMEM(state.shape, jnp.float32),
            pltpu.VMEM(load_rate.shape, jnp.int32),
            pltpu.VMEM(near_band.shape, jnp.bfloat16),
            pltpu.VMEM((cols,) + u_far.shape, jnp.bfloat16),
            pltpu.VMEM((cols,) + v_far.shape, jnp.bfloat16),
            pltpu.VMEM((3, rows, members, own), jnp.bfloat16),
            dma((6,)),
            dma((2, cols)),
            dma((2, cols)),
            dma((3, chips)),
            dma((3, chips)),
            dma((3, chips)),
            dma((3, chips)),
        ],
        compiler_params=pltpu.CompilerParams(
            collective_id=0, has_side_effects=True, vmem_limit_bytes=48 * 1024 * 1024
        ),
        cost_estimate=pl.CostEstimate(flops=400_000_000, bytes_accessed=4_000_000, transcendentals=300_000),
    )(stress, state, load_rate, a_param, b_param, near_band, u_far, v_far, ranks)


def solution(mesh):
    return jax.shard_map(
        local,
        mesh=mesh,
        in_specs=(
            P("col", "row"),
            P("col", "row"),
            P("col", "row"),
            P("row"),
            P("row"),
            P("row", None),
            P("row", "col", None, None),
            P("row", "col", None, None),
            P("row", "col"),
        ),
        out_specs=(P("col", "row"), P("col", "row")),
        check_vma=False,
    )
```

```python
import functools

import jax
import jax.numpy as jnp
from jax import lax
from jax.experimental import pallas as pl
from jax.experimental.pallas import tpu as pltpu
from jax.sharding import PartitionSpec as P

B = 128
HSTEP = 0.2
RATE_UNIT = 1.0 / 1024.0
MESH = pl.DeviceIdType.MESH


def partner(index, step, count):
    assert count & (count - 1) == 0
    bit = 1
    while bit <= step:
        if step & bit:
            index = index + bit - 2 * bit * ((index // bit) % 2)
        bit *= 2
    return index


def dot_t(left, right):
    return lax.dot_general(left, right, (((1,), (1,)), ((), ())), preferred_element_type=jnp.float32)


def kernel(
    rows,
    cols,
    stress_in,
    state_in,
    load_in,
    a_hbm,
    b_hbm,
    band_in,
    u_in,
    v_in,
    ranks_hbm,
    stress_out,
    state_out,
    stress0,
    state0,
    load,
    a_in,
    b_in,
    ranks,
    band,
    u_all,
    v_all,
    grid,
    load_sem,
    w_send,
    w_recv,
    g_send,
    g_recv,
    f_send,
    f_recv,
):
    row = lax.axis_index("row")
    col = lax.axis_index("col")
    chips = rows // 2
    chip = row // 2
    core = row % 2
    peer = 2 * chip + 1 - core
    _, block_rows, block_cols, slots, dofs = u_all.shape
    members = stress0.shape[0]

    barrier = pltpu.get_barrier_semaphore()
    others = [(row, partner(col, t, cols)) for t in ([1, 2] if cols == 4 else range(1, cols))]
    others += [(2 * partner(chip, t, chips) + core, col) for t in range(1, chips)]
    others += [(peer, col)]
    for other in others:
        pl.semaphore_signal(barrier, inc=1, device_id=other, device_id_type=MESH)

    loads = [
        pltpu.make_async_copy(source, target, load_sem.at[n])
        for n, (source, target) in enumerate(
            [
                (ranks_hbm, ranks),
                (u_in, u_all.at[col]),
                (stress_in, stress0),
                (state_in, state0),
                (a_hbm, a_in),
                (b_hbm, b_in),
                (load_in, load),
                (v_in, v_all.at[col]),
                (band_in, band),
            ]
        )
    ]
    for copy in loads:
        copy.start()

    loads[0].wait()
    loads[1].wait()
    slot = lax.broadcasted_iota(jnp.int32, (slots, dofs), 0)
    for i in range(block_rows):
        for j in range(block_cols):
            spacing = jnp.abs(row * block_rows + i - col * block_cols - j)
            limit = jnp.where(spacing >= 2, ranks[i, j], 0)
            factors = u_all[col, i, j].astype(jnp.float32)
            u_all[col, i, j] = jnp.where(slot < limit, factors, 0.0).astype(jnp.bfloat16)

    pl.semaphore_wait(barrier, len(others))

    def send(source, target, send_sem, recv_sem, device):
        copy = pltpu.make_async_remote_copy(
            src_ref=source,
            dst_ref=target,
            send_sem=send_sem,
            recv_sem=recv_sem,
            device_id=device,
            device_id_type=MESH,
        )
        copy.start()
        return copy

    sent = []
    relayed = cols == 4
    col_steps = [1, 2] if relayed else list(range(1, cols))

    def send_factors(kind, source, owner, t, to):
        target = (v_all, u_all)[kind].at[owner]
        copy = send(source, target, w_send.at[kind, t], w_recv.at[kind, t], (row, partner(col, to, cols)))
        sent.append(copy)
        return copy

    v_copies = {t: send_factors(0, v_in, col, t, t) for t in col_steps}
    u_copies = {}

    def send_u():
        for t in col_steps:
            u_copies[t] = send_factors(1, u_all.at[col], col, t, t)

    def relay_v():
        if relayed:
            v_copies[1].wait_recv()
            owner = partner(col, 1, cols)
            v_copies[3] = send_factors(0, v_all.at[owner], owner, 3, 2)

    def relay_u():
        if relayed:
            u_copies[2].wait_recv()
            owner = partner(col, 2, cols)
            u_copies[3] = send_factors(1, u_all.at[owner], owner, 3, 1)

    def wait_factors(copies, t):
        if not (relayed and t == (1 if copies is v_copies else 2)):
            copies[t].wait_recv()

    def weights(s, j):
        parts = []
        per_row = block_cols // 2
        for n in range(block_cols):
            excess = grid[s, 2 * j + n // per_row, :, (n % per_row) * dofs : (n % per_row + 1) * dofs]
            factors = v_all[j, :, n].reshape(block_rows * slots, dofs)
            parts.append(dot_t(excess, factors).astype(jnp.bfloat16))
        return [
            jnp.concatenate([part[:, i * slots : (i + 1) * slots] for part in parts], axis=1)
            for i in range(block_rows)
        ]

    def far(j, weight):
        return [
            jnp.dot(
                weight[i], u_all[j, i].reshape(block_cols * slots, dofs), preferred_element_type=jnp.float32
            )
            for i in range(block_rows)
        ]

    def band_tile(i, n):
        return band[i * dofs : (i + 1) * dofs, n * dofs : (n + 1) * dofs]

    def section(s, stress_now, state_now):
        drift = []
        for i in range(block_rows):
            lanes = slice(i * B, (i + 1) * B)
            theta = state_now[:, lanes]
            direct = a_in[lanes].reshape(1, B)
            squares = None
            for d in range(2):
                dof = slice((2 * i + d) * B, (2 * i + d + 1) * B)
                scaled = stress_now[:, dof] / direct
                rate = jnp.exp(scaled - theta) - jnp.exp(-scaled - theta)
                plate = load[:, dof].astype(jnp.float32) * RATE_UNIT
                grid[s, row, :, dof] = (rate - plate).astype(jnp.bfloat16)
                squares = rate * rate if squares is None else squares + rate * rate
            drift.append((theta, squares, b_in[lanes].reshape(1, B)))
        mine = grid.at[s, row]
        order = list(range(2, chips)) + [1] if chips > 1 else []
        g_copies = {}
        f_copies = {0: send(mine, mine, f_send.at[s, 0], f_recv.at[s, 0], (peer, col))}
        for t in order:
            g_copies[t] = send(
                mine, mine, g_send.at[s, t], g_recv.at[s, t], (2 * partner(chip, t, chips) + core, col)
            )
        if s == 0:
            relay_v()
            send_u()
            loads[7].wait()
            loads[8].wait()
        drift = jnp.concatenate(
            [evolve * (jnp.exp(-theta) - jnp.sqrt(squares)) for theta, squares, evolve in drift], axis=1
        )

        total = [None] * block_rows
        for i in range(block_rows):
            for n in range(max(i - 1, 0), min(i + 2, block_rows)):
                term = dot_t(grid[s, row, :, n * dofs : (n + 1) * dofs], band_tile(i, n - i + 1))
                total[i] = term if total[i] is None else total[i] + term

        def add(terms):
            for i in range(block_rows):
                total[i] = total[i] + terms[i]

        def relay(t):
            g_copies[t].wait_recv()
            got = grid.at[s, 2 * partner(chip, t, chips) + core]
            f_copies[t] = send(got, got, f_send.at[s, t], f_recv.at[s, t], (peer, col))

        f_copies[0].wait_recv()
        if s == 0:
            for t in range(1, chips):
                relay(t)
            for t in range(1, chips):
                f_copies[t].wait_recv()
            relay_u()
            ready = [(col, weights(s, col))]
            for t in range(1, cols):
                wait_factors(v_copies, t)
                j = partner(col, t, cols)
                ready.append((j, weights(s, j)))
            for t, (j, weight) in enumerate(ready):
                if t > 0:
                    wait_factors(u_copies, t)
                add(far(j, weight))
        else:
            for t in range(1, chips):
                relay(t)
                if t > 1:
                    f_copies[t - 1].wait_recv()
                j = partner(chip, t - 1, chips)
                add(far(j, weights(s, j)))
            if chips > 1:
                f_copies[chips - 1].wait_recv()
            j = partner(chip, chips - 1, chips)
            add(far(j, weights(s, j)))

        left = grid[s, (row + rows - 1) % rows, :, (block_rows - 1) * dofs :]
        right = grid[s, (row + 1) % rows, :, :dofs]
        left_term = dot_t(left, band_tile(0, 0))
        right_term = dot_t(right, band_tile(block_rows - 1, 2))
        total[0] = total[0] + jnp.where(row > 0, left_term, 0.0)
        total[-1] = total[-1] + jnp.where(row < rows - 1, right_term, 0.0)
        sent.extend(g_copies.values())
        sent.extend(f_copies.values())
        return -jnp.concatenate(total, axis=1), drift

    for copy in loads[2:7]:
        copy.wait()
    rate, drift = section(0, stress0[...], state0[...])
    stress_out[...] = stress0[...] + HSTEP * rate
    state_out[...] = state0[...] + HSTEP * drift
    rate, drift = section(1, stress_out[...], state_out[...])
    stress_out[...] = 0.75 * stress0[...] + 0.25 * (stress_out[...] + HSTEP * rate)
    state_out[...] = 0.75 * state0[...] + 0.25 * (state_out[...] + HSTEP * drift)
    rate, drift = section(2, stress_out[...], state_out[...])
    stress_out[...] = stress0[...] / 3.0 + 2.0 / 3.0 * (stress_out[...] + HSTEP * rate)
    state_out[...] = state0[...] / 3.0 + 2.0 / 3.0 * (state_out[...] + HSTEP * drift)
    for copy in sent:
        copy.wait_send()


def local(stress, state, load_rate, a_param, b_param, near_band, u_far, v_far, ranks):
    rows = lax.axis_size("row")
    cols = lax.axis_size("col")
    members, own = stress.shape
    chips = rows // 2
    hbm = pl.BlockSpec(memory_space=pltpu.HBM)
    vmem = pl.BlockSpec(memory_space=pltpu.VMEM)
    dma = pltpu.SemaphoreType.DMA
    return pl.pallas_call(
        functools.partial(kernel, rows, cols),
        out_shape=(
            jax.ShapeDtypeStruct(stress.shape, jnp.float32),
            jax.ShapeDtypeStruct(state.shape, jnp.float32),
        ),
        in_specs=[hbm] * 9,
        out_specs=(vmem, vmem),
        scratch_shapes=[
            pltpu.VMEM(stress.shape, jnp.float32),
            pltpu.VMEM(state.shape, jnp.float32),
            pltpu.VMEM(load_rate.shape, jnp.int32),
            pltpu.VMEM(a_param.shape, jnp.float32),
            pltpu.VMEM(b_param.shape, jnp.float32),
            pltpu.SMEM(ranks.shape, jnp.int32),
            pltpu.VMEM(near_band.shape, jnp.bfloat16),
            pltpu.VMEM((cols,) + u_far.shape, jnp.bfloat16),
            pltpu.VMEM((cols,) + v_far.shape, jnp.bfloat16),
            pltpu.VMEM((3, rows, members, own), jnp.bfloat16),
            dma((9,)),
            dma((2, cols)),
            dma((2, cols)),
            dma((3, chips)),
            dma((3, chips)),
            dma((3, chips)),
            dma((3, chips)),
        ],
        compiler_params=pltpu.CompilerParams(
            collective_id=0, has_side_effects=True, vmem_limit_bytes=60 * 1024 * 1024
        ),
        cost_estimate=pl.CostEstimate(flops=400_000_000, bytes_accessed=4_000_000, transcendentals=300_000),
    )(stress, state, load_rate, a_param, b_param, near_band, u_far, v_far, ranks)


def solution(mesh):
    return jax.shard_map(
        local,
        mesh=mesh,
        in_specs=(
            P("col", "row"),
            P("col", "row"),
            P("col", "row"),
            P("row"),
            P("row"),
            P("row", None),
            P("row", "col", None, None),
            P("row", "col", None, None),
            P("row", "col"),
        ),
        out_specs=(P("col", "row"), P("col", "row")),
        check_vma=False,
    )
```

```python
import functools

import jax
import jax.numpy as jnp
from jax import lax
from jax.experimental import pallas as pl
from jax.experimental.pallas import tpu as pltpu
from jax.sharding import PartitionSpec as P

B = 128
HSTEP = 0.2
RATE_UNIT = 1.0 / 1024.0
MESH = pl.DeviceIdType.MESH


def partner(index, step, count):
    assert count & (count - 1) == 0
    bit = 1
    while bit <= step:
        if step & bit:
            index = index + bit - 2 * bit * ((index // bit) % 2)
        bit *= 2
    return index


def kernel(
    rows,
    cols,
    stress_in,
    state_in,
    load_in,
    a_hbm,
    b_hbm,
    band_in,
    u_in,
    v_in,
    ranks_hbm,
    stress_out,
    state_out,
    stress0,
    state0,
    load,
    a_in,
    b_in,
    ranks,
    band,
    u_all,
    v_all,
    v_own,
    band_t,
    grid,
    load_sem,
    w_send,
    w_recv,
    g_send,
    g_recv,
    f_send,
    f_recv,
):
    row = lax.axis_index("row")
    col = lax.axis_index("col")
    chips = rows // 2
    chip = row // 2
    core = row % 2
    peer = 2 * chip + 1 - core
    _, block_rows, block_cols, slots, dofs = u_all.shape
    _, halves, _, half, _ = grid.shape

    barrier = pltpu.get_barrier_semaphore()
    others = [(row, partner(col, t, cols)) for t in ([1, 2] if cols == 4 else range(1, cols))]
    others += [(2 * partner(chip, t, chips) + core, col) for t in range(1, chips)]
    others += [(peer, col)]
    for other in others:
        pl.semaphore_signal(barrier, inc=1, device_id=other, device_id_type=MESH)

    loads = [
        pltpu.make_async_copy(source, target, load_sem.at[n])
        for n, (source, target) in enumerate(
            [
                (ranks_hbm, ranks),
                (v_in, v_own),
                (u_in, u_all.at[col]),
                (stress_in, stress0),
                (state_in, state0),
                (a_hbm, a_in),
                (b_hbm, b_in),
                (load_in, load),
                (band_in, band),
            ]
        )
    ]
    for copy in loads:
        copy.start()

    loads[1].wait()
    v_all[col] = v_own[...].reshape(block_rows * block_cols * slots, dofs).T

    pl.semaphore_wait(barrier, len(others))

    def send(source, target, send_sem, recv_sem, device):
        copy = pltpu.make_async_remote_copy(
            src_ref=source,
            dst_ref=target,
            send_sem=send_sem,
            recv_sem=recv_sem,
            device_id=device,
            device_id_type=MESH,
        )
        copy.start()
        return copy

    sent = []
    relayed = cols == 4
    col_steps = [1, 2] if relayed else list(range(1, cols))

    def send_factors(kind, source, owner, t, to):
        target = (v_all, u_all)[kind].at[owner]
        copy = send(source, target, w_send.at[kind, t], w_recv.at[kind, t], (row, partner(col, to, cols)))
        sent.append(copy)
        return copy

    v_copies = {t: send_factors(0, v_all.at[col], col, t, t) for t in col_steps}
    u_copies = {}

    def send_u():
        for t in col_steps:
            u_copies[t] = send_factors(1, u_all.at[col], col, t, t)

    def relay_v():
        if relayed:
            v_copies[1].wait_recv()
            owner = partner(col, 1, cols)
            v_copies[3] = send_factors(0, v_all.at[owner], owner, 3, 2)

    def relay_u():
        if relayed:
            u_copies[2].wait_recv()
            owner = partner(col, 2, cols)
            u_copies[3] = send_factors(1, u_all.at[owner], owner, 3, 1)

    def wait_factors(copies, t):
        if not (relayed and t == (1 if copies is v_copies else 2)):
            copies[t].wait_recv()

    def mask_u():
        loads[0].wait()
        loads[2].wait()
        slot = lax.broadcasted_iota(jnp.int32, (slots, dofs), 0)
        for i in range(block_rows):
            for j in range(block_cols):
                spacing = jnp.abs(row * block_rows + i - col * block_cols - j)
                limit = jnp.where(spacing >= 2, ranks[i, j], 0)
                factors = u_all[col, i, j].astype(jnp.float32)
                u_all[col, i, j] = jnp.where(slot < limit, factors, 0.0).astype(jnp.bfloat16)

    def weights(s, h, j):
        per_row = block_cols // 2
        blocks = [
            grid[s, h, 2 * j + n // per_row, :, (n % per_row) * dofs : (n % per_row + 1) * dofs]
            for n in range(block_cols)
        ]
        products = jnp.dot(
            jnp.concatenate(blocks, axis=0), v_all[j], preferred_element_type=jnp.float32
        )
        lane = lax.broadcasted_iota(jnp.int32, (half, block_rows * block_cols * slots), 1)
        owner = (lane // slots) % block_cols
        weight = products[:half]
        for n in range(1, block_cols):
            weight = jnp.where(owner == n, products[n * half : (n + 1) * half], weight)
        return weight.astype(jnp.bfloat16)

    def far(j, weight):
        width = block_cols * slots
        return [
            jnp.dot(
                weight[:, i * width : (i + 1) * width],
                u_all[j, i].reshape(width, dofs),
                preferred_element_type=jnp.float32,
            )
            for i in range(block_rows)
        ]

    def added(total, terms):
        return [old + term for old, term in zip(total, terms)]

    def near_own(s, h):
        total = [None] * block_rows
        for i in range(block_rows):
            for n in range(max(i - 1, 0), min(i + 2, block_rows)):
                term = jnp.dot(
                    grid[s, h, row, :, n * dofs : (n + 1) * dofs],
                    band_t[i, n - i + 1],
                    preferred_element_type=jnp.float32,
                )
                total[i] = term if total[i] is None else total[i] + term
        return total

    def near_edges(s, h, total):
        left = grid[s, h, (row + rows - 1) % rows, :, (block_rows - 1) * dofs :]
        right = grid[s, h, (row + 1) % rows, :, :dofs]
        left_term = jnp.dot(left, band_t[0, 0], preferred_element_type=jnp.float32)
        right_term = jnp.dot(right, band_t[block_rows - 1, 2], preferred_element_type=jnp.float32)
        total = list(total)
        total[0] = total[0] + jnp.where(row > 0, left_term, 0.0)
        total[-1] = total[-1] + jnp.where(row < rows - 1, right_term, 0.0)
        return total

    g_copies = {}
    f_copies = {}

    def stepped(s, start, now, rate):
        if s == 0:
            return start + HSTEP * rate
        if s == 1:
            return 0.75 * start + 0.25 * (now + HSTEP * rate)
        return start / 3.0 + 2.0 / 3.0 * (now + HSTEP * rate)

    def excess(s, h):
        members_now = slice(h * half, (h + 1) * half)
        stress_now, state_now = (stress0, state0) if s == 0 else (stress_out, state_out)
        later = []
        for i in range(block_rows):
            lanes = slice(i * B, (i + 1) * B)
            theta = state_now[members_now, lanes]
            direct = a_in[lanes].reshape(1, B)
            squares = None
            for d in range(2):
                dof = slice((2 * i + d) * B, (2 * i + d + 1) * B)
                scaled = stress_now[members_now, dof] / direct
                rate = jnp.exp(scaled - theta) - jnp.exp(-scaled - theta)
                plate = load[members_now, dof].astype(jnp.float32) * RATE_UNIT
                grid[s, h, row, :, dof] = (rate - plate).astype(jnp.bfloat16)
                squares = rate * rate if squares is None else squares + rate * rate
            later.append((lanes, theta, squares))
        mine = grid.at[s, h, row]
        f_copies[s, h, 0] = send(mine, mine, f_send.at[s, h, 0], f_recv.at[s, h, 0], (peer, col))
        for t in list(range(2, chips)) + list(range(1, min(2, chips))):
            g_copies[s, h, t] = send(
                mine,
                mine,
                g_send.at[s, h, t],
                g_recv.at[s, h, t],
                (2 * partner(chip, t, chips) + core, col),
            )
        for lanes, theta, squares in later:
            drift = b_in[lanes].reshape(1, B) * (jnp.exp(-theta) - jnp.sqrt(squares))
            state_out[members_now, lanes] = stepped(s, state0[members_now, lanes], theta, drift)

    def relay(s, h, t):
        g_copies[s, h, t].wait_recv()
        got = grid.at[s, h, 2 * partner(chip, t, chips) + core]
        f_copies[s, h, t] = send(got, got, f_send.at[s, h, t], f_recv.at[s, h, t], (peer, col))

    def finish(s, h, total):
        members_now = slice(h * half, (h + 1) * half)
        stress_now = stress0 if s == 0 else stress_out
        for i in range(block_rows):
            lanes = slice(i * dofs, (i + 1) * dofs)
            stress_out[members_now, lanes] = stepped(
                s, stress0[members_now, lanes], stress_now[members_now, lanes], -total[i]
            )

    for copy in loads[3:8]:
        copy.wait()
    for h in range(halves):
        excess(0, h)
    mask_u()
    relay_v()
    send_u()
    loads[8].wait()
    for i in range(block_rows):
        for n in range(3):
            band_t[i, n] = band[i * dofs : (i + 1) * dofs, n * dofs : (n + 1) * dofs].T
    for h in range(halves):
        for t in range(1, chips):
            relay(0, h, t)
    totals = [near_own(0, h) for h in range(halves)]
    for h in range(halves):
        for t in range(chips):
            f_copies[0, h, t].wait_recv()
        totals[h] = near_edges(0, h, totals[h])
    relay_u()
    ready = []
    for t in range(cols):
        j = partner(col, t, cols)
        if t > 0:
            wait_factors(v_copies, t)
        ready.append((j, [weights(0, h, j) for h in range(halves)]))
    for t, (j, weight) in enumerate(ready):
        if t > 0:
            wait_factors(u_copies, t)
        for h in range(halves):
            totals[h] = added(totals[h], far(j, weight[h]))
            if t == cols - 1:
                finish(0, h, totals[h])
                excess(1, h)

    for s in (1, 2):
        for h in range(halves):
            total = near_own(s, h)
            f_copies[s, h, 0].wait_recv()
            for t in range(1, chips):
                relay(s, h, t)
                if t > 1:
                    f_copies[s, h, t - 1].wait_recv()
                j = partner(chip, t - 1, chips)
                total = added(total, far(j, weights(s, h, j)))
            if chips > 1:
                f_copies[s, h, chips - 1].wait_recv()
            j = partner(chip, chips - 1, chips)
            total = added(total, far(j, weights(s, h, j)))
            finish(s, h, near_edges(s, h, total))
            if s == 1:
                excess(2, h)

    for copy in sent + list(g_copies.values()) + list(f_copies.values()):
        copy.wait_send()


def local(stress, state, load_rate, a_param, b_param, near_band, u_far, v_far, ranks):
    rows = lax.axis_size("row")
    cols = lax.axis_size("col")
    members, own = stress.shape
    block_rows, block_cols, slots, dofs = u_far.shape
    chips = rows // 2
    halves = 2 if members % 32 == 0 else 1
    hbm = pl.BlockSpec(memory_space=pltpu.HBM)
    vmem = pl.BlockSpec(memory_space=pltpu.VMEM)
    dma = pltpu.SemaphoreType.DMA
    return pl.pallas_call(
        functools.partial(kernel, rows, cols),
        out_shape=(
            jax.ShapeDtypeStruct(stress.shape, jnp.float32),
            jax.ShapeDtypeStruct(state.shape, jnp.float32),
        ),
        in_specs=[hbm] * 9,
        out_specs=(vmem, vmem),
        scratch_shapes=[
            pltpu.VMEM(stress.shape, jnp.float32),
            pltpu.VMEM(state.shape, jnp.float32),
            pltpu.VMEM(load_rate.shape, jnp.int32),
            pltpu.VMEM(a_param.shape, jnp.float32),
            pltpu.VMEM(b_param.shape, jnp.float32),
            pltpu.SMEM(ranks.shape, jnp.int32),
            pltpu.VMEM(near_band.shape, jnp.bfloat16),
            pltpu.VMEM((cols,) + u_far.shape, jnp.bfloat16),
            pltpu.VMEM((cols, dofs, block_rows * block_cols * slots), jnp.bfloat16),
            pltpu.VMEM(v_far.shape, jnp.bfloat16),
            pltpu.VMEM((block_rows, 3, dofs, dofs), jnp.bfloat16),
            pltpu.VMEM((3, halves, rows, members // halves, own), jnp.bfloat16),
            dma((9,)),
            dma((2, cols)),
            dma((2, cols)),
            dma((3, halves, chips)),
            dma((3, halves, chips)),
            dma((3, halves, chips)),
            dma((3, halves, chips)),
        ],
        compiler_params=pltpu.CompilerParams(
            collective_id=0, has_side_effects=True, vmem_limit_bytes=60 * 1024 * 1024
        ),
        cost_estimate=pl.CostEstimate(flops=400_000_000, bytes_accessed=4_000_000, transcendentals=300_000),
    )(stress, state, load_rate, a_param, b_param, near_band, u_far, v_far, ranks)


def solution(mesh):
    return jax.shard_map(
        local,
        mesh=mesh,
        in_specs=(
            P("col", "row"),
            P("col", "row"),
            P("col", "row"),
            P("row"),
            P("row"),
            P("row", None),
            P("row", "col", None, None),
            P("row", "col", None, None),
            P("row", "col"),
        ),
        out_specs=(P("col", "row"), P("col", "row")),
        check_vma=False,
    )
```

```python
import functools

import jax
import jax.numpy as jnp
from jax import lax
from jax.experimental import pallas as pl
from jax.experimental.pallas import tpu as pltpu
from jax.sharding import PartitionSpec as P

B = 128
HSTEP = 0.2
RATE_UNIT = 1.0 / 1024.0
MESH = pl.DeviceIdType.MESH


def partner(index, step, count):
    assert count & (count - 1) == 0
    bit = 1
    while bit <= step:
        if step & bit:
            index = index + bit - 2 * bit * ((index // bit) % 2)
        bit *= 2
    return index


def kernel(
    rows,
    cols,
    stress_in,
    state_in,
    load_in,
    a_hbm,
    b_hbm,
    band_in,
    u_in,
    v_in,
    ranks_hbm,
    stress_out,
    state_out,
    stress0,
    state0,
    load,
    a_in,
    b_in,
    ranks,
    band,
    u_all,
    v_all,
    v_own,
    band_t,
    grid,
    load_sem,
    w_send,
    w_recv,
    g_send,
    g_recv,
    f_send,
    f_recv,
):
    row = lax.axis_index("row")
    col = lax.axis_index("col")
    chips = rows // 2
    chip = row // 2
    core = row % 2
    peer = 2 * chip + 1 - core
    _, block_rows, block_cols, slots, dofs = u_all.shape
    _, halves, _, half, _ = grid.shape

    barrier = pltpu.get_barrier_semaphore()
    others = [(row, partner(col, t, cols)) for t in ([1, 2] if cols == 4 else range(1, cols))]
    others += [(2 * partner(chip, t, chips) + core, col) for t in range(1, chips)]
    others += [(peer, col)]
    for other in others:
        pl.semaphore_signal(barrier, inc=1, device_id=other, device_id_type=MESH)

    loads = [
        pltpu.make_async_copy(source, target, load_sem.at[n])
        for n, (source, target) in enumerate(
            [
                (ranks_hbm, ranks),
                (v_in, v_own),
                (u_in, u_all.at[col]),
                (stress_in, stress0),
                (state_in, state0),
                (a_hbm, a_in),
                (b_hbm, b_in),
                (load_in, load),
                (band_in, band),
            ]
        )
    ]
    for copy in loads:
        copy.start()

    loads[1].wait()
    v_all[col] = v_own[...].reshape(block_rows * block_cols * slots, dofs).T

    pl.semaphore_wait(barrier, len(others))

    def send(source, target, send_sem, recv_sem, device):
        copy = pltpu.make_async_remote_copy(
            src_ref=source,
            dst_ref=target,
            send_sem=send_sem,
            recv_sem=recv_sem,
            device_id=device,
            device_id_type=MESH,
        )
        copy.start()
        return copy

    sent = []
    relayed = cols == 4
    col_steps = [1, 2] if relayed else list(range(1, cols))

    def send_factors(kind, source, owner, t, to):
        target = (v_all, u_all)[kind].at[owner]
        copy = send(source, target, w_send.at[kind, t], w_recv.at[kind, t], (row, partner(col, to, cols)))
        sent.append(copy)
        return copy

    v_copies = {t: send_factors(0, v_all.at[col], col, t, t) for t in col_steps}
    u_copies = {}

    def send_u():
        for t in col_steps:
            u_copies[t] = send_factors(1, u_all.at[col], col, t, t)

    def relay_v():
        if relayed:
            v_copies[1].wait_recv()
            owner = partner(col, 1, cols)
            v_copies[3] = send_factors(0, v_all.at[owner], owner, 3, 2)

    def relay_u():
        if relayed:
            u_copies[2].wait_recv()
            owner = partner(col, 2, cols)
            u_copies[3] = send_factors(1, u_all.at[owner], owner, 3, 1)

    def wait_factors(copies, t):
        if not (relayed and t == (1 if copies is v_copies else 2)):
            copies[t].wait_recv()

    def mask_u():
        loads[0].wait()
        loads[2].wait()
        slot = lax.broadcasted_iota(jnp.int32, (slots, dofs), 0)
        for i in range(block_rows):
            for j in range(block_cols):
                spacing = jnp.abs(row * block_rows + i - col * block_cols - j)
                limit = jnp.where(spacing >= 2, ranks[i, j], 0)
                factors = u_all[col, i, j].astype(jnp.float32)
                u_all[col, i, j] = jnp.where(slot < limit, factors, 0.0).astype(jnp.bfloat16)

    def weights(s, h, j):
        per_row = block_cols // 2
        blocks = [
            grid[s, h, 2 * j + n // per_row, :, (n % per_row) * dofs : (n % per_row + 1) * dofs]
            for n in range(block_cols)
        ]
        products = jnp.dot(
            jnp.concatenate(blocks, axis=0), v_all[j], preferred_element_type=jnp.float32
        )
        lane = lax.broadcasted_iota(jnp.int32, (half, block_rows * block_cols * slots), 1)
        owner = (lane // slots) % block_cols
        weight = products[:half]
        for n in range(1, block_cols):
            weight = jnp.where(owner == n, products[n * half : (n + 1) * half], weight)
        return weight.astype(jnp.bfloat16)

    def far(j, weight):
        width = block_cols * slots
        return [
            jnp.dot(
                weight[:, i * width : (i + 1) * width],
                u_all[j, i].reshape(width, dofs),
                preferred_element_type=jnp.float32,
            )
            for i in range(block_rows)
        ]

    def added(total, terms):
        return [old + term for old, term in zip(total, terms)]

    def near_own(s, h):
        total = [None] * block_rows
        for i in range(block_rows):
            for n in range(max(i - 1, 0), min(i + 2, block_rows)):
                term = jnp.dot(
                    grid[s, h, row, :, n * dofs : (n + 1) * dofs],
                    band_t[i, n - i + 1],
                    preferred_element_type=jnp.float32,
                )
                total[i] = term if total[i] is None else total[i] + term
        return total

    def near_edges(s, h, total):
        left = grid[s, h, (row + rows - 1) % rows, :, (block_rows - 1) * dofs :]
        right = grid[s, h, (row + 1) % rows, :, :dofs]
        left_term = jnp.dot(left, band_t[0, 0], preferred_element_type=jnp.float32)
        right_term = jnp.dot(right, band_t[block_rows - 1, 2], preferred_element_type=jnp.float32)
        total = list(total)
        total[0] = total[0] + jnp.where(row > 0, left_term, 0.0)
        total[-1] = total[-1] + jnp.where(row < rows - 1, right_term, 0.0)
        return total

    g_copies = {}
    f_copies = {}
    left_for = set()
    order = list(range(2, chips)) + list(range(1, min(2, chips)))

    def leave(key):
        if key not in left_for:
            left_for.add(key)
            for t in order:
                g_copies[key + (t,)].wait_send()

    def stepped(s, start, now, rate):
        if s == 0:
            return start + HSTEP * rate
        if s == 1:
            return 0.75 * start + 0.25 * (now + HSTEP * rate)
        return start / 3.0 + 2.0 / 3.0 * (now + HSTEP * rate)

    def spread(s, h):
        mine = grid.at[s, h, row]
        for t in order:
            g_copies[s, h, t] = send(
                mine,
                mine,
                g_send.at[s, h, t],
                g_recv.at[s, h, t],
                (2 * partner(chip, t, chips) + core, col),
            )

    def excess(s, h, at_once):
        members_now = slice(h * half, (h + 1) * half)
        stress_now, state_now = (stress0, state0) if s == 0 else (stress_out, state_out)
        later = []
        for i in range(block_rows):
            lanes = slice(i * B, (i + 1) * B)
            theta = state_now[members_now, lanes]
            direct = a_in[lanes].reshape(1, B)
            squares = None
            for d in range(2):
                dof = slice((2 * i + d) * B, (2 * i + d + 1) * B)
                scaled = stress_now[members_now, dof] / direct
                rate = jnp.exp(scaled - theta) - jnp.exp(-scaled - theta)
                plate = load[members_now, dof].astype(jnp.float32) * RATE_UNIT
                grid[s, h, row, :, dof] = (rate - plate).astype(jnp.bfloat16)
                squares = rate * rate if squares is None else squares + rate * rate
            later.append((lanes, theta, squares))
        mine = grid.at[s, h, row]
        f_copies[s, h, 0] = send(mine, mine, f_send.at[s, h, 0], f_recv.at[s, h, 0], (peer, col))
        if at_once:
            spread(s, h)
        for lanes, theta, squares in later:
            drift = b_in[lanes].reshape(1, B) * (jnp.exp(-theta) - jnp.sqrt(squares))
            state_out[members_now, lanes] = stepped(s, state0[members_now, lanes], theta, drift)

    def relay(s, h, t):
        g_copies[s, h, t].wait_recv()
        got = grid.at[s, h, 2 * partner(chip, t, chips) + core]
        f_copies[s, h, t] = send(got, got, f_send.at[s, h, t], f_recv.at[s, h, t], (peer, col))

    def finish(s, h, total):
        members_now = slice(h * half, (h + 1) * half)
        stress_now = stress0 if s == 0 else stress_out
        for i in range(block_rows):
            lanes = slice(i * dofs, (i + 1) * dofs)
            stress_out[members_now, lanes] = stepped(
                s, stress0[members_now, lanes], stress_now[members_now, lanes], -total[i]
            )

    for copy in loads[3:8]:
        copy.wait()
    for h in range(halves):
        excess(0, h, True)
    mask_u()
    relay_v()
    send_u()
    loads[8].wait()
    for i in range(block_rows):
        for n in range(3):
            band_t[i, n] = band[i * dofs : (i + 1) * dofs, n * dofs : (n + 1) * dofs].T
    for h in range(halves):
        for t in order:
            relay(0, h, t)
    totals = [near_own(0, h) for h in range(halves)]
    for h in range(halves):
        for t in range(chips):
            f_copies[0, h, t].wait_recv()
        totals[h] = near_edges(0, h, totals[h])
    relay_u()
    ready = []
    for t in range(cols):
        j = partner(col, t, cols)
        if t > 0:
            wait_factors(v_copies, t)
        ready.append((j, [weights(0, h, j) for h in range(halves)]))
    for t, (j, weight) in enumerate(ready):
        if t > 0:
            wait_factors(u_copies, t)
        for h in range(halves):
            totals[h] = added(totals[h], far(j, weight[h]))
            if t == cols - 1:
                finish(0, h, totals[h])
                excess(1, h, h == 0)

    turns = [(s, h) for s in (1, 2) for h in range(halves)]
    for n, (s, h) in enumerate(turns):
        total = near_own(s, h)
        f_copies[s, h, 0].wait_recv()
        behind = 0
        for m, t in enumerate(order):
            relay(s, h, t)
            if halves > 1 and m == max(len(order) - 2, 0) and n + 1 < len(turns):
                leave((s, h))
                spread(*turns[n + 1])
            if behind > 0:
                f_copies[s, h, behind].wait_recv()
            j = partner(chip, behind, chips)
            total = added(total, far(j, weights(s, h, j)))
            behind = t
        if behind > 0:
            f_copies[s, h, behind].wait_recv()
        j = partner(chip, behind, chips)
        total = added(total, far(j, weights(s, h, j)))
        finish(s, h, near_edges(s, h, total))
        if s == 1:
            excess(2, h, halves == 1)

    for s in range(3):
        for h in range(halves):
            leave((s, h))
    for copy in sent + list(f_copies.values()):
        copy.wait_send()


def local(stress, state, load_rate, a_param, b_param, near_band, u_far, v_far, ranks):
    rows = lax.axis_size("row")
    cols = lax.axis_size("col")
    members, own = stress.shape
    block_rows, block_cols, slots, dofs = u_far.shape
    chips = rows // 2
    halves = 2 if members % 32 == 0 else 1
    hbm = pl.BlockSpec(memory_space=pltpu.HBM)
    vmem = pl.BlockSpec(memory_space=pltpu.VMEM)
    dma = pltpu.SemaphoreType.DMA
    return pl.pallas_call(
        functools.partial(kernel, rows, cols),
        out_shape=(
            jax.ShapeDtypeStruct(stress.shape, jnp.float32),
            jax.ShapeDtypeStruct(state.shape, jnp.float32),
        ),
        in_specs=[hbm] * 9,
        out_specs=(vmem, vmem),
        scratch_shapes=[
            pltpu.VMEM(stress.shape, jnp.float32),
            pltpu.VMEM(state.shape, jnp.float32),
            pltpu.VMEM(load_rate.shape, jnp.int32),
            pltpu.VMEM(a_param.shape, jnp.float32),
            pltpu.VMEM(b_param.shape, jnp.float32),
            pltpu.SMEM(ranks.shape, jnp.int32),
            pltpu.VMEM(near_band.shape, jnp.bfloat16),
            pltpu.VMEM((cols,) + u_far.shape, jnp.bfloat16),
            pltpu.VMEM((cols, dofs, block_rows * block_cols * slots), jnp.bfloat16),
            pltpu.VMEM(v_far.shape, jnp.bfloat16),
            pltpu.VMEM((block_rows, 3, dofs, dofs), jnp.bfloat16),
            pltpu.VMEM((3, halves, rows, members // halves, own), jnp.bfloat16),
            dma((9,)),
            dma((2, cols)),
            dma((2, cols)),
            dma((3, halves, chips)),
            dma((3, halves, chips)),
            dma((3, halves, chips)),
            dma((3, halves, chips)),
        ],
        compiler_params=pltpu.CompilerParams(
            collective_id=0, has_side_effects=True, vmem_limit_bytes=60 * 1024 * 1024
        ),
        cost_estimate=pl.CostEstimate(flops=400_000_000, bytes_accessed=4_000_000, transcendentals=300_000),
    )(stress, state, load_rate, a_param, b_param, near_band, u_far, v_far, ranks)


def solution(mesh):
    return jax.shard_map(
        local,
        mesh=mesh,
        in_specs=(
            P("col", "row"),
            P("col", "row"),
            P("col", "row"),
            P("row"),
            P("row"),
            P("row", None),
            P("row", "col", None, None),
            P("row", "col", None, None),
            P("row", "col"),
        ),
        out_specs=(P("col", "row"), P("col", "row")),
        check_vma=False,
    )
```

```python
import functools

import jax
import jax.numpy as jnp
from jax import lax
from jax.experimental import pallas as pl
from jax.experimental.pallas import tpu as pltpu
from jax.sharding import PartitionSpec as P

B = 128
HSTEP = 0.2
RATE_UNIT = 1.0 / 1024.0
MESH = pl.DeviceIdType.MESH


def partner(index, step, count):
    assert count & (count - 1) == 0
    bit = 1
    while bit <= step:
        if step & bit:
            index = index + bit - 2 * bit * ((index // bit) % 2)
        bit *= 2
    return index


def kernel(
    rows,
    cols,
    stress_in,
    state_in,
    load_in,
    a_hbm,
    b_hbm,
    band_in,
    u_in,
    v_in,
    ranks_hbm,
    stress_out,
    state_out,
    stress0,
    state0,
    load,
    a_in,
    b_in,
    ranks,
    band,
    u_all,
    v_all,
    v_own,
    band_t,
    grid,
    load_sem,
    w_send,
    w_recv,
    g_send,
    g_recv,
    f_send,
    f_recv,
):
    row = lax.axis_index("row")
    col = lax.axis_index("col")
    chips = rows // 2
    chip = row // 2
    core = row % 2
    peer = 2 * chip + 1 - core
    _, block_rows, block_cols, slots, dofs = u_all.shape
    _, halves, _, half, _ = grid.shape

    barrier = pltpu.get_barrier_semaphore()
    others = [(row, partner(col, t, cols)) for t in ([1, 2] if cols == 4 else range(1, cols))]
    others += [(2 * partner(chip, t, chips) + core, col) for t in range(1, chips)]
    others += [(peer, col)]
    for other in others:
        pl.semaphore_signal(barrier, inc=1, device_id=other, device_id_type=MESH)

    loads = [
        pltpu.make_async_copy(source, target, load_sem.at[n])
        for n, (source, target) in enumerate(
            [
                (ranks_hbm, ranks),
                (v_in, v_own),
                (u_in, u_all.at[col]),
                (stress_in, stress0),
                (state_in, state0),
                (a_hbm, a_in),
                (b_hbm, b_in),
                (load_in, load),
                (band_in, band),
            ]
        )
    ]
    for copy in loads:
        copy.start()

    loads[1].wait()
    v_all[col] = v_own[...].reshape(block_rows * block_cols * slots, dofs).T

    pl.semaphore_wait(barrier, len(others))

    def send(source, target, send_sem, recv_sem, device):
        copy = pltpu.make_async_remote_copy(
            src_ref=source,
            dst_ref=target,
            send_sem=send_sem,
            recv_sem=recv_sem,
            device_id=device,
            device_id_type=MESH,
        )
        copy.start()
        return copy

    sent = []
    relayed = cols == 4
    col_steps = [1, 2] if relayed else list(range(1, cols))

    def send_factors(kind, source, owner, t, to):
        target = (v_all, u_all)[kind].at[owner]
        copy = send(source, target, w_send.at[kind, t], w_recv.at[kind, t], (row, partner(col, to, cols)))
        sent.append(copy)
        return copy

    v_copies = {t: send_factors(0, v_all.at[col], col, t, t) for t in col_steps}
    u_copies = {}

    def send_u():
        for t in col_steps:
            u_copies[t] = send_factors(1, u_all.at[col], col, t, t)

    def relay_v():
        if relayed:
            v_copies[1].wait_recv()
            owner = partner(col, 1, cols)
            v_copies[3] = send_factors(0, v_all.at[owner], owner, 3, 2)

    def relay_u():
        if relayed:
            u_copies[2].wait_recv()
            owner = partner(col, 2, cols)
            u_copies[3] = send_factors(1, u_all.at[owner], owner, 3, 1)

    def wait_factors(copies, t):
        if not (relayed and t == (1 if copies is v_copies else 2)):
            copies[t].wait_recv()

    def mask_u():
        loads[0].wait()
        loads[2].wait()
        slot = lax.broadcasted_iota(jnp.int32, (slots, dofs), 0)
        for i in range(block_rows):
            for j in range(block_cols):
                spacing = jnp.abs(row * block_rows + i - col * block_cols - j)
                limit = jnp.where(spacing >= 2, ranks[i, j], 0)
                factors = u_all[col, i, j].astype(jnp.float32)
                u_all[col, i, j] = jnp.where(slot < limit, factors, 0.0).astype(jnp.bfloat16)

    def weights(s, h, j):
        per_row = block_cols // 2
        blocks = [
            grid[s, h, 2 * j + n // per_row, :, (n % per_row) * dofs : (n % per_row + 1) * dofs]
            for n in range(block_cols)
        ]
        products = jnp.dot(
            jnp.concatenate(blocks, axis=0), v_all[j], preferred_element_type=jnp.float32
        )
        lane = lax.broadcasted_iota(jnp.int32, (half, block_rows * block_cols * slots), 1)
        owner = (lane // slots) % block_cols
        weight = products[:half]
        for n in range(1, block_cols):
            weight = jnp.where(owner == n, products[n * half : (n + 1) * half], weight)
        return weight.astype(jnp.bfloat16)

    def far(j, weight):
        width = block_cols * slots
        return [
            jnp.dot(
                weight[:, i * width : (i + 1) * width],
                u_all[j, i].reshape(width, dofs),
                preferred_element_type=jnp.float32,
            )
            for i in range(block_rows)
        ]

    def added(total, terms):
        return [old + term for old, term in zip(total, terms)]

    def near_own(s, h):
        total = [None] * block_rows
        for i in range(block_rows):
            for n in range(max(i - 1, 0), min(i + 2, block_rows)):
                term = jnp.dot(
                    grid[s, h, row, :, n * dofs : (n + 1) * dofs],
                    band_t[i, n - i + 1],
                    preferred_element_type=jnp.float32,
                )
                total[i] = term if total[i] is None else total[i] + term
        return total

    def near_edges(s, h, total):
        left = grid[s, h, (row + rows - 1) % rows, :, (block_rows - 1) * dofs :]
        right = grid[s, h, (row + 1) % rows, :, :dofs]
        left_term = jnp.dot(left, band_t[0, 0], preferred_element_type=jnp.float32)
        right_term = jnp.dot(right, band_t[block_rows - 1, 2], preferred_element_type=jnp.float32)
        total = list(total)
        total[0] = total[0] + jnp.where(row > 0, left_term, 0.0)
        total[-1] = total[-1] + jnp.where(row < rows - 1, right_term, 0.0)
        return total

    g_copies = {}
    f_copies = {}
    left_for = set()
    order = list(range(2, chips)) + list(range(1, min(2, chips)))

    def leave(key):
        if key not in left_for:
            left_for.add(key)
            for t in order:
                g_copies[key + (t,)].wait_send()

    def stepped(s, start, now, rate):
        if s == 0:
            return start + HSTEP * rate
        if s == 1:
            return 0.75 * start + 0.25 * (now + HSTEP * rate)
        return start / 3.0 + 2.0 / 3.0 * (now + HSTEP * rate)

    def spread(s, h):
        mine = grid.at[s, h, row]
        for t in order:
            g_copies[s, h, t] = send(
                mine,
                mine,
                g_send.at[s, h, t],
                g_recv.at[s, h, t],
                (2 * partner(chip, t, chips) + core, col),
            )

    def excess(s, h, at_once):
        members_now = slice(h * half, (h + 1) * half)
        stress_now, state_now = (stress0, state0) if s == 0 else (stress_out, state_out)
        later = []
        for i in range(block_rows):
            lanes = slice(i * B, (i + 1) * B)
            theta = state_now[members_now, lanes]
            direct = a_in[lanes].reshape(1, B)
            squares = None
            for d in range(2):
                dof = slice((2 * i + d) * B, (2 * i + d + 1) * B)
                scaled = stress_now[members_now, dof] / direct
                rate = jnp.exp(scaled - theta) - jnp.exp(-scaled - theta)
                plate = load[members_now, dof].astype(jnp.float32) * RATE_UNIT
                grid[s, h, row, :, dof] = (rate - plate).astype(jnp.bfloat16)
                squares = rate * rate if squares is None else squares + rate * rate
            later.append((lanes, theta, squares))
        mine = grid.at[s, h, row]
        f_copies[s, h, 0] = send(mine, mine, f_send.at[s, h, 0], f_recv.at[s, h, 0], (peer, col))
        if at_once:
            spread(s, h)
        for lanes, theta, squares in later:
            drift = b_in[lanes].reshape(1, B) * (jnp.exp(-theta) - jnp.sqrt(squares))
            state_out[members_now, lanes] = stepped(s, state0[members_now, lanes], theta, drift)

    def relay(s, h, t):
        g_copies[s, h, t].wait_recv()
        got = grid.at[s, h, 2 * partner(chip, t, chips) + core]
        f_copies[s, h, t] = send(got, got, f_send.at[s, h, t], f_recv.at[s, h, t], (peer, col))

    def finish(s, h, total):
        members_now = slice(h * half, (h + 1) * half)
        stress_now = stress0 if s == 0 else stress_out
        for i in range(block_rows):
            lanes = slice(i * dofs, (i + 1) * dofs)
            stress_out[members_now, lanes] = stepped(
                s, stress0[members_now, lanes], stress_now[members_now, lanes], -total[i]
            )

    for copy in loads[3:8]:
        copy.wait()
    for h in range(halves):
        excess(0, h, True)
    mask_u()
    relay_v()
    send_u()
    loads[8].wait()
    for i in range(block_rows):
        for n in range(3):
            band_t[i, n] = band[i * dofs : (i + 1) * dofs, n * dofs : (n + 1) * dofs].T
    for h in range(halves):
        for t in range(1, chips):
            relay(0, h, t)
    totals = [near_own(0, h) for h in range(halves)]
    for h in range(halves):
        for t in range(chips):
            f_copies[0, h, t].wait_recv()
        totals[h] = near_edges(0, h, totals[h])
    relay_u()
    ready = []
    for t in range(cols):
        j = partner(col, t, cols)
        if t > 0:
            wait_factors(v_copies, t)
        ready.append((j, [weights(0, h, j) for h in range(halves)]))
    for t, (j, weight) in enumerate(ready):
        if t > 0:
            wait_factors(u_copies, t)
        for h in range(halves):
            totals[h] = added(totals[h], far(j, weight[h]))
            if t == cols - 1:
                finish(0, h, totals[h])
                excess(1, h, h == 0)

    turns = [(s, h) for s in (1, 2) for h in range(halves)]
    for n, (s, h) in enumerate(turns):
        total = near_own(s, h)
        f_copies[s, h, 0].wait_recv()
        behind = 0
        for m, t in enumerate(range(1, chips)):
            relay(s, h, t)
            if halves > 1 and m == max(len(order) - 2, 0) and n + 1 < len(turns):
                leave((s, h))
                spread(*turns[n + 1])
            if behind > 0:
                f_copies[s, h, behind].wait_recv()
            j = partner(chip, behind, chips)
            total = added(total, far(j, weights(s, h, j)))
            behind = t
        if behind > 0:
            f_copies[s, h, behind].wait_recv()
        j = partner(chip, behind, chips)
        total = added(total, far(j, weights(s, h, j)))
        finish(s, h, near_edges(s, h, total))
        if s == 1:
            excess(2, h, halves == 1)

    for s in range(3):
        for h in range(halves):
            leave((s, h))
    for copy in sent + list(f_copies.values()):
        copy.wait_send()


def local(stress, state, load_rate, a_param, b_param, near_band, u_far, v_far, ranks):
    rows = lax.axis_size("row")
    cols = lax.axis_size("col")
    members, own = stress.shape
    block_rows, block_cols, slots, dofs = u_far.shape
    chips = rows // 2
    halves = 1
    hbm = pl.BlockSpec(memory_space=pltpu.HBM)
    vmem = pl.BlockSpec(memory_space=pltpu.VMEM)
    dma = pltpu.SemaphoreType.DMA
    return pl.pallas_call(
        functools.partial(kernel, rows, cols),
        out_shape=(
            jax.ShapeDtypeStruct(stress.shape, jnp.float32),
            jax.ShapeDtypeStruct(state.shape, jnp.float32),
        ),
        in_specs=[hbm] * 9,
        out_specs=(vmem, vmem),
        scratch_shapes=[
            pltpu.VMEM(stress.shape, jnp.float32),
            pltpu.VMEM(state.shape, jnp.float32),
            pltpu.VMEM(load_rate.shape, jnp.int32),
            pltpu.VMEM(a_param.shape, jnp.float32),
            pltpu.VMEM(b_param.shape, jnp.float32),
            pltpu.SMEM(ranks.shape, jnp.int32),
            pltpu.VMEM(near_band.shape, jnp.bfloat16),
            pltpu.VMEM((cols,) + u_far.shape, jnp.bfloat16),
            pltpu.VMEM((cols, dofs, block_rows * block_cols * slots), jnp.bfloat16),
            pltpu.VMEM(v_far.shape, jnp.bfloat16),
            pltpu.VMEM((block_rows, 3, dofs, dofs), jnp.bfloat16),
            pltpu.VMEM((3, halves, rows, members // halves, own), jnp.bfloat16),
            dma((9,)),
            dma((2, cols)),
            dma((2, cols)),
            dma((3, halves, chips)),
            dma((3, halves, chips)),
            dma((3, halves, chips)),
            dma((3, halves, chips)),
        ],
        compiler_params=pltpu.CompilerParams(
            collective_id=0, has_side_effects=True, vmem_limit_bytes=60 * 1024 * 1024
        ),
        cost_estimate=pl.CostEstimate(flops=400_000_000, bytes_accessed=4_000_000, transcendentals=300_000),
    )(stress, state, load_rate, a_param, b_param, near_band, u_far, v_far, ranks)


def solution(mesh):
    return jax.shard_map(
        local,
        mesh=mesh,
        in_specs=(
            P("col", "row"),
            P("col", "row"),
            P("col", "row"),
            P("row"),
            P("row"),
            P("row", None),
            P("row", "col", None, None),
            P("row", "col", None, None),
            P("row", "col"),
        ),
        out_specs=(P("col", "row"), P("col", "row")),
        check_vma=False,
    )
```

```python
import functools

import jax
import jax.numpy as jnp
from jax import lax
from jax.experimental import pallas as pl
from jax.experimental.pallas import tpu as pltpu
from jax.sharding import PartitionSpec as P

B = 128
HSTEP = 0.2
RATE_UNIT = 1.0 / 1024.0
MESH = pl.DeviceIdType.MESH


def partner(index, step, count):
    assert count & (count - 1) == 0
    bit = 1
    while bit <= step:
        if step & bit:
            index = index + bit - 2 * bit * ((index // bit) % 2)
        bit *= 2
    return index


def kernel(
    rows,
    cols,
    stress_in,
    state_in,
    load_in,
    a_hbm,
    b_hbm,
    band_in,
    u_in,
    v_in,
    ranks_hbm,
    stress_out,
    state_out,
    stress0,
    state0,
    load,
    a_in,
    b_in,
    ranks,
    band,
    u_all,
    v_all,
    v_own,
    band_t,
    grid,
    load_sem,
    w_send,
    w_recv,
    g_send,
    g_recv,
    f_send,
    f_recv,
):
    row = lax.axis_index("row")
    col = lax.axis_index("col")
    chips = rows // 2
    chip = row // 2
    core = row % 2
    peer = 2 * chip + 1 - core
    _, block_rows, block_cols, slots, dofs = u_all.shape
    _, halves, _, half, _ = grid.shape

    barrier = pltpu.get_barrier_semaphore()
    others = [(row, partner(col, t, cols)) for t in ([1, 2] if cols == 4 else range(1, cols))]
    others += [(2 * partner(chip, t, chips) + core, col) for t in range(1, chips)]
    others += [(peer, col)]
    for other in others:
        pl.semaphore_signal(barrier, inc=1, device_id=other, device_id_type=MESH)

    loads = [
        pltpu.make_async_copy(source, target, load_sem.at[n])
        for n, (source, target) in enumerate(
            [
                (ranks_hbm, ranks),
                (v_in, v_own),
                (u_in, u_all.at[col]),
                (stress_in, stress0),
                (state_in, state0),
                (a_hbm, a_in),
                (b_hbm, b_in),
                (load_in, load),
                (band_in, band),
            ]
        )
    ]
    for copy in loads:
        copy.start()

    loads[1].wait()
    v_all[col] = v_own[...].reshape(block_rows * block_cols * slots, dofs).T

    pl.semaphore_wait(barrier, len(others))

    def send(source, target, send_sem, recv_sem, device):
        copy = pltpu.make_async_remote_copy(
            src_ref=source,
            dst_ref=target,
            send_sem=send_sem,
            recv_sem=recv_sem,
            device_id=device,
            device_id_type=MESH,
        )
        copy.start()
        return copy

    sent = []
    relayed = cols == 4
    col_steps = [1, 2] if relayed else list(range(1, cols))

    def send_factors(kind, source, owner, t, to):
        target = (v_all, u_all)[kind].at[owner]
        copy = send(source, target, w_send.at[kind, t], w_recv.at[kind, t], (row, partner(col, to, cols)))
        sent.append(copy)
        return copy

    v_copies = {t: send_factors(0, v_all.at[col], col, t, t) for t in col_steps}
    u_copies = {}

    def send_u():
        for t in col_steps:
            u_copies[t] = send_factors(1, u_all.at[col], col, t, t)

    def relay_v():
        if relayed:
            v_copies[1].wait_recv()
            owner = partner(col, 1, cols)
            v_copies[3] = send_factors(0, v_all.at[owner], owner, 3, 2)

    def relay_u():
        if relayed:
            u_copies[2].wait_recv()
            owner = partner(col, 2, cols)
            u_copies[3] = send_factors(1, u_all.at[owner], owner, 3, 1)

    def wait_factors(copies, t):
        if not (relayed and t == (1 if copies is v_copies else 2)):
            copies[t].wait_recv()

    def mask_u():
        loads[0].wait()
        loads[2].wait()
        slot = lax.broadcasted_iota(jnp.int32, (slots, dofs), 0)
        for i in range(block_rows):
            for j in range(block_cols):
                spacing = jnp.abs(row * block_rows + i - col * block_cols - j)
                limit = jnp.where(spacing >= 2, ranks[i, j], 0)
                factors = u_all[col, i, j].astype(jnp.float32)
                u_all[col, i, j] = jnp.where(slot < limit, factors, 0.0).astype(jnp.bfloat16)

    def weights(s, h, j):
        per_row = block_cols // 2
        blocks = [
            grid[s, h, 2 * j + n // per_row, :, (n % per_row) * dofs : (n % per_row + 1) * dofs]
            for n in range(block_cols)
        ]
        products = jnp.dot(
            jnp.concatenate(blocks, axis=0), v_all[j], preferred_element_type=jnp.float32
        )
        lane = lax.broadcasted_iota(jnp.int32, (half, block_rows * block_cols * slots), 1)
        owner = (lane // slots) % block_cols
        weight = products[:half]
        for n in range(1, block_cols):
            weight = jnp.where(owner == n, products[n * half : (n + 1) * half], weight)
        return weight.astype(jnp.bfloat16)

    def far(j, weight):
        width = block_cols * slots
        return [
            jnp.dot(
                weight[:, i * width : (i + 1) * width],
                u_all[j, i].reshape(width, dofs),
                preferred_element_type=jnp.float32,
            )
            for i in range(block_rows)
        ]

    def added(total, terms):
        return [old + term for old, term in zip(total, terms)]

    def near_own(s, h):
        total = [None] * block_rows
        for i in range(block_rows):
            for n in range(max(i - 1, 0), min(i + 2, block_rows)):
                term = jnp.dot(
                    grid[s, h, row, :, n * dofs : (n + 1) * dofs],
                    band_t[i, n - i + 1],
                    preferred_element_type=jnp.float32,
                )
                total[i] = term if total[i] is None else total[i] + term
        return total

    def near_edges(s, h, total):
        left = grid[s, h, (row + rows - 1) % rows, :, (block_rows - 1) * dofs :]
        right = grid[s, h, (row + 1) % rows, :, :dofs]
        left_term = jnp.dot(left, band_t[0, 0], preferred_element_type=jnp.float32)
        right_term = jnp.dot(right, band_t[block_rows - 1, 2], preferred_element_type=jnp.float32)
        total = list(total)
        total[0] = total[0] + jnp.where(row > 0, left_term, 0.0)
        total[-1] = total[-1] + jnp.where(row < rows - 1, right_term, 0.0)
        return total

    g_copies = {}
    f_copies = {}

    def stepped(s, start, now, rate):
        if s == 0:
            return start + HSTEP * rate
        if s == 1:
            return 0.75 * start + 0.25 * (now + HSTEP * rate)
        return start / 3.0 + 2.0 / 3.0 * (now + HSTEP * rate)

    def excess(s, h):
        members_now = slice(h * half, (h + 1) * half)
        stress_now, state_now = (stress0, state0) if s == 0 else (stress_out, state_out)
        later = []
        for i in range(block_rows):
            lanes = slice(i * B, (i + 1) * B)
            theta = state_now[members_now, lanes]
            direct = a_in[lanes].reshape(1, B)
            squares = None
            for d in range(2):
                dof = slice((2 * i + d) * B, (2 * i + d + 1) * B)
                scaled = stress_now[members_now, dof] / direct
                rate = jnp.exp(scaled - theta) - jnp.exp(-scaled - theta)
                plate = load[members_now, dof].astype(jnp.float32) * RATE_UNIT
                grid[s, h, row, :, dof] = (rate - plate).astype(jnp.bfloat16)
                squares = rate * rate if squares is None else squares + rate * rate
            later.append((lanes, theta, squares))
        mine = grid.at[s, h, row]
        f_copies[s, h, 0] = send(mine, mine, f_send.at[s, h, 0], f_recv.at[s, h, 0], (peer, col))
        for t in list(range(2, chips)) + list(range(1, min(2, chips))):
            g_copies[s, h, t] = send(
                mine,
                mine,
                g_send.at[s, h, t],
                g_recv.at[s, h, t],
                (2 * partner(chip, t, chips) + core, col),
            )
        for lanes, theta, squares in later:
            drift = b_in[lanes].reshape(1, B) * (jnp.exp(-theta) - jnp.sqrt(squares))
            state_out[members_now, lanes] = stepped(s, state0[members_now, lanes], theta, drift)

    def relay(s, h, t):
        g_copies[s, h, t].wait_recv()
        got = grid.at[s, h, 2 * partner(chip, t, chips) + core]
        f_copies[s, h, t] = send(got, got, f_send.at[s, h, t], f_recv.at[s, h, t], (peer, col))

    def finish(s, h, total):
        members_now = slice(h * half, (h + 1) * half)
        stress_now = stress0 if s == 0 else stress_out
        for i in range(block_rows):
            lanes = slice(i * dofs, (i + 1) * dofs)
            stress_out[members_now, lanes] = stepped(
                s, stress0[members_now, lanes], stress_now[members_now, lanes], -total[i]
            )

    for copy in loads[3:8]:
        copy.wait()
    for h in range(halves):
        excess(0, h)
    mask_u()
    send_u()
    relay_v()
    loads[8].wait()
    for i in range(block_rows):
        for n in range(3):
            band_t[i, n] = band[i * dofs : (i + 1) * dofs, n * dofs : (n + 1) * dofs].T
    relay_u()
    for h in range(halves):
        for t in range(1, chips):
            relay(0, h, t)
    totals = [near_own(0, h) for h in range(halves)]
    for h in range(halves):
        for t in range(chips):
            f_copies[0, h, t].wait_recv()
        totals[h] = near_edges(0, h, totals[h])
    ready = []
    for t in range(cols):
        j = partner(col, t, cols)
        if t > 0:
            wait_factors(v_copies, t)
        ready.append((j, [weights(0, h, j) for h in range(halves)]))
    for t, (j, weight) in enumerate(ready):
        if t > 0:
            wait_factors(u_copies, t)
        for h in range(halves):
            totals[h] = added(totals[h], far(j, weight[h]))
            if t == cols - 1:
                finish(0, h, totals[h])
                excess(1, h)

    for s in (1, 2):
        for h in range(halves):
            total = near_own(s, h)
            f_copies[s, h, 0].wait_recv()
            for t in range(1, chips):
                relay(s, h, t)
                if t > 1:
                    f_copies[s, h, t - 1].wait_recv()
                j = partner(chip, t - 1, chips)
                total = added(total, far(j, weights(s, h, j)))
            if chips > 1:
                f_copies[s, h, chips - 1].wait_recv()
            j = partner(chip, chips - 1, chips)
            total = added(total, far(j, weights(s, h, j)))
            finish(s, h, near_edges(s, h, total))
            if s == 1:
                excess(2, h)

    for copy in sent + list(g_copies.values()) + list(f_copies.values()):
        copy.wait_send()


def hand_out(stress_in, state_in, stress_out, state_out, sems):
    copies = [
        pltpu.make_async_copy(stress_in, stress_out, sems.at[0]),
        pltpu.make_async_copy(state_in, state_out, sems.at[1]),
    ]
    for copy in copies:
        copy.start()
    for copy in copies:
        copy.wait()


def local(stress, state, load_rate, a_param, b_param, near_band, u_far, v_far, ranks):
    rows = lax.axis_size("row")
    cols = lax.axis_size("col")
    members, own = stress.shape
    block_rows, block_cols, slots, dofs = u_far.shape
    chips = rows // 2
    halves = 2 if members % 32 == 0 else 1
    hbm = pl.BlockSpec(memory_space=pltpu.HBM)
    vmem = pl.BlockSpec(memory_space=pltpu.VMEM)
    dma = pltpu.SemaphoreType.DMA
    results = (
        jax.ShapeDtypeStruct(stress.shape, jnp.float32),
        jax.ShapeDtypeStruct(state.shape, jnp.float32),
    )
    stepped = pl.pallas_call(
        functools.partial(kernel, rows, cols),
        out_shape=results,
        in_specs=[hbm] * 9,
        out_specs=(vmem, vmem),
        scratch_shapes=[
            pltpu.VMEM(stress.shape, jnp.float32),
            pltpu.VMEM(state.shape, jnp.float32),
            pltpu.VMEM(load_rate.shape, jnp.int32),
            pltpu.VMEM(a_param.shape, jnp.float32),
            pltpu.VMEM(b_param.shape, jnp.float32),
            pltpu.SMEM(ranks.shape, jnp.int32),
            pltpu.VMEM(near_band.shape, jnp.bfloat16),
            pltpu.VMEM((cols,) + u_far.shape, jnp.bfloat16),
            pltpu.VMEM((cols, dofs, block_rows * block_cols * slots), jnp.bfloat16),
            pltpu.VMEM(v_far.shape, jnp.bfloat16),
            pltpu.VMEM((block_rows, 3, dofs, dofs), jnp.bfloat16),
            pltpu.VMEM((3, halves, rows, members // halves, own), jnp.bfloat16),
            dma((9,)),
            dma((2, cols)),
            dma((2, cols)),
            dma((3, halves, chips)),
            dma((3, halves, chips)),
            dma((3, halves, chips)),
            dma((3, halves, chips)),
        ],
        compiler_params=pltpu.CompilerParams(
            collective_id=0, has_side_effects=True, vmem_limit_bytes=60 * 1024 * 1024
        ),
        cost_estimate=pl.CostEstimate(flops=400_000_000, bytes_accessed=4_000_000, transcendentals=300_000),
    )(stress, state, load_rate, a_param, b_param, near_band, u_far, v_far, ranks)
    anywhere = pl.BlockSpec(memory_space=pl.ANY)
    return pl.pallas_call(
        hand_out,
        out_shape=results,
        in_specs=[anywhere] * 2,
        out_specs=(anywhere, anywhere),
        scratch_shapes=[dma((2,))],
        compiler_params=pltpu.CompilerParams(vmem_limit_bytes=60 * 1024 * 1024),
        cost_estimate=pl.CostEstimate(flops=0, bytes_accessed=400_000, transcendentals=0),
    )(*stepped)


def solution(mesh):
    return jax.shard_map(
        local,
        mesh=mesh,
        in_specs=(
            P("col", "row"),
            P("col", "row"),
            P("col", "row"),
            P("row"),
            P("row"),
            P("row", None),
            P("row", "col", None, None),
            P("row", "col", None, None),
            P("row", "col"),
        ),
        out_specs=(P("col", "row"), P("col", "row")),
        check_vma=False,
    )
```

```python
import functools

import jax
import jax.numpy as jnp
from jax import lax
from jax.experimental import pallas as pl
from jax.experimental.pallas import tpu as pltpu
from jax.sharding import PartitionSpec as P

B = 128
HSTEP = 0.2
RATE_UNIT = 1.0 / 1024.0
MESH = pl.DeviceIdType.MESH


def partner(index, step, count):
    assert count & (count - 1) == 0
    bit = 1
    while bit <= step:
        if step & bit:
            index = index + bit - 2 * bit * ((index // bit) % 2)
        bit *= 2
    return index


def kernel(
    rows,
    cols,
    stress_in,
    state_in,
    load_in,
    a_hbm,
    b_hbm,
    band_in,
    u_in,
    v_in,
    ranks_hbm,
    stress_out,
    state_out,
    stress0,
    state0,
    load,
    a_in,
    b_in,
    ranks,
    band,
    u_all,
    v_all,
    v_own,
    band_t,
    grid,
    load_sem,
    w_send,
    w_recv,
    g_send,
    g_recv,
    f_send,
    f_recv,
):
    row = lax.axis_index("row")
    col = lax.axis_index("col")
    chips = rows // 2
    chip = row // 2
    core = row % 2
    peer = 2 * chip + 1 - core
    _, block_rows, block_cols, slots, dofs = u_all.shape
    _, halves, _, half, _ = grid.shape

    barrier = pltpu.get_barrier_semaphore()
    others = [(row, partner(col, t, cols)) for t in ([1, 2] if cols == 4 else range(1, cols))]
    others += [(2 * partner(chip, t, chips) + core, col) for t in range(1, chips)]
    others += [(peer, col)]
    for other in others:
        pl.semaphore_signal(barrier, inc=1, device_id=other, device_id_type=MESH)

    loads = [
        pltpu.make_async_copy(source, target, load_sem.at[n])
        for n, (source, target) in enumerate(
            [
                (ranks_hbm, ranks),
                (v_in, v_own),
                (u_in, u_all.at[col]),
                (stress_in, stress0),
                (state_in, state0),
                (a_hbm, a_in),
                (b_hbm, b_in),
                (load_in, load),
                (band_in, band),
            ]
        )
    ]
    for copy in loads:
        copy.start()

    loads[1].wait()
    v_all[col] = v_own[...].reshape(block_rows * block_cols * slots, dofs).T

    pl.semaphore_wait(barrier, len(others))

    def send(source, target, send_sem, recv_sem, device):
        copy = pltpu.make_async_remote_copy(
            src_ref=source,
            dst_ref=target,
            send_sem=send_sem,
            recv_sem=recv_sem,
            device_id=device,
            device_id_type=MESH,
        )
        copy.start()
        return copy

    sent = []
    relayed = cols == 4
    col_steps = [1, 2] if relayed else list(range(1, cols))

    def send_factors(kind, source, owner, t, to):
        target = (v_all, u_all)[kind].at[owner]
        copy = send(source, target, w_send.at[kind, t], w_recv.at[kind, t], (row, partner(col, to, cols)))
        sent.append(copy)
        return copy

    v_copies = {}
    u_copies = {}

    def send_first():
        for t in [1] if relayed else col_steps:
            v_copies[t] = send_factors(0, v_all.at[col], col, t, t)
        if relayed:
            u_copies[2] = send_factors(1, u_all.at[col], col, 2, 2)

    def send_second():
        if relayed:
            v_copies[2] = send_factors(0, v_all.at[col], col, 2, 2)
        for t in [1] if relayed else col_steps:
            u_copies[t] = send_factors(1, u_all.at[col], col, t, t)

    def relay_v():
        if relayed:
            v_copies[1].wait_recv()
            owner = partner(col, 1, cols)
            v_copies[3] = send_factors(0, v_all.at[owner], owner, 3, 2)

    def relay_u():
        if relayed:
            u_copies[2].wait_recv()
            owner = partner(col, 2, cols)
            u_copies[3] = send_factors(1, u_all.at[owner], owner, 3, 1)

    def wait_factors(copies, t):
        if not (relayed and t == (1 if copies is v_copies else 2)):
            copies[t].wait_recv()

    def mask_u():
        loads[0].wait()
        loads[2].wait()
        slot = lax.broadcasted_iota(jnp.int32, (slots, dofs), 0)
        for i in range(block_rows):
            for j in range(block_cols):
                spacing = jnp.abs(row * block_rows + i - col * block_cols - j)
                limit = jnp.where(spacing >= 2, ranks[i, j], 0)
                factors = u_all[col, i, j].astype(jnp.float32)
                u_all[col, i, j] = jnp.where(slot < limit, factors, 0.0).astype(jnp.bfloat16)

    def weights(s, h, j):
        per_row = block_cols // 2
        blocks = [
            grid[s, h, 2 * j + n // per_row, :, (n % per_row) * dofs : (n % per_row + 1) * dofs]
            for n in range(block_cols)
        ]
        products = jnp.dot(
            jnp.concatenate(blocks, axis=0), v_all[j], preferred_element_type=jnp.float32
        )
        lane = lax.broadcasted_iota(jnp.int32, (half, block_rows * block_cols * slots), 1)
        owner = (lane // slots) % block_cols
        weight = products[:half]
        for n in range(1, block_cols):
            weight = jnp.where(owner == n, products[n * half : (n + 1) * half], weight)
        return weight.astype(jnp.bfloat16)

    def far(j, weight):
        width = block_cols * slots
        return [
            jnp.dot(
                weight[:, i * width : (i + 1) * width],
                u_all[j, i].reshape(width, dofs),
                preferred_element_type=jnp.float32,
            )
            for i in range(block_rows)
        ]

    def added(total, terms):
        return [old + term for old, term in zip(total, terms)]

    def near_own(s, h):
        total = [None] * block_rows
        for i in range(block_rows):
            for n in range(max(i - 1, 0), min(i + 2, block_rows)):
                term = jnp.dot(
                    grid[s, h, row, :, n * dofs : (n + 1) * dofs],
                    band_t[i, n - i + 1],
                    preferred_element_type=jnp.float32,
                )
                total[i] = term if total[i] is None else total[i] + term
        return total

    def near_edges(s, h, total):
        left = grid[s, h, (row + rows - 1) % rows, :, (block_rows - 1) * dofs :]
        right = grid[s, h, (row + 1) % rows, :, :dofs]
        left_term = jnp.dot(left, band_t[0, 0], preferred_element_type=jnp.float32)
        right_term = jnp.dot(right, band_t[block_rows - 1, 2], preferred_element_type=jnp.float32)
        total = list(total)
        total[0] = total[0] + jnp.where(row > 0, left_term, 0.0)
        total[-1] = total[-1] + jnp.where(row < rows - 1, right_term, 0.0)
        return total

    g_copies = {}
    f_copies = {}

    def stepped(s, start, now, rate):
        if s == 0:
            return start + HSTEP * rate
        if s == 1:
            return 0.75 * start + 0.25 * (now + HSTEP * rate)
        return start / 3.0 + 2.0 / 3.0 * (now + HSTEP * rate)

    def excess(s, h):
        members_now = slice(h * half, (h + 1) * half)
        stress_now, state_now = (stress0, state0) if s == 0 else (stress_out, state_out)
        later = []
        for i in range(block_rows):
            lanes = slice(i * B, (i + 1) * B)
            theta = state_now[members_now, lanes]
            direct = a_in[lanes].reshape(1, B)
            squares = None
            for d in range(2):
                dof = slice((2 * i + d) * B, (2 * i + d + 1) * B)
                scaled = stress_now[members_now, dof] / direct
                rate = jnp.exp(scaled - theta) - jnp.exp(-scaled - theta)
                plate = load[members_now, dof].astype(jnp.float32) * RATE_UNIT
                grid[s, h, row, :, dof] = (rate - plate).astype(jnp.bfloat16)
                squares = rate * rate if squares is None else squares + rate * rate
            later.append((lanes, theta, squares))
        mine = grid.at[s, h, row]
        f_copies[s, h, 0] = send(mine, mine, f_send.at[s, h, 0], f_recv.at[s, h, 0], (peer, col))
        for t in list(range(2, chips)) + list(range(1, min(2, chips))):
            g_copies[s, h, t] = send(
                mine,
                mine,
                g_send.at[s, h, t],
                g_recv.at[s, h, t],
                (2 * partner(chip, t, chips) + core, col),
            )
        for lanes, theta, squares in later:
            drift = b_in[lanes].reshape(1, B) * (jnp.exp(-theta) - jnp.sqrt(squares))
            state_out[members_now, lanes] = stepped(s, state0[members_now, lanes], theta, drift)

    def relay(s, h, t):
        g_copies[s, h, t].wait_recv()
        got = grid.at[s, h, 2 * partner(chip, t, chips) + core]
        f_copies[s, h, t] = send(got, got, f_send.at[s, h, t], f_recv.at[s, h, t], (peer, col))

    def finish(s, h, total):
        members_now = slice(h * half, (h + 1) * half)
        stress_now = stress0 if s == 0 else stress_out
        for i in range(block_rows):
            lanes = slice(i * dofs, (i + 1) * dofs)
            stress_out[members_now, lanes] = stepped(
                s, stress0[members_now, lanes], stress_now[members_now, lanes], -total[i]
            )

    mask_u()
    send_first()
    for copy in loads[3:8]:
        copy.wait()
    for h in range(halves):
        excess(0, h)
    send_second()
    relay_v()
    relay_u()
    loads[8].wait()
    for i in range(block_rows):
        for n in range(3):
            band_t[i, n] = band[i * dofs : (i + 1) * dofs, n * dofs : (n + 1) * dofs].T
    for h in range(halves):
        for t in range(1, chips):
            relay(0, h, t)
    totals = [near_own(0, h) for h in range(halves)]
    for h in range(halves):
        for t in range(chips):
            f_copies[0, h, t].wait_recv()
        totals[h] = near_edges(0, h, totals[h])
    ready = []
    for t in range(cols):
        j = partner(col, t, cols)
        if t > 0:
            wait_factors(v_copies, t)
        ready.append((j, [weights(0, h, j) for h in range(halves)]))
    for t, (j, weight) in enumerate(ready):
        if t > 0:
            wait_factors(u_copies, t)
        for h in range(halves):
            totals[h] = added(totals[h], far(j, weight[h]))
            if t == cols - 1:
                finish(0, h, totals[h])
                excess(1, h)

    for s in (1, 2):
        for h in range(halves):
            total = near_own(s, h)
            f_copies[s, h, 0].wait_recv()
            for t in range(1, chips):
                relay(s, h, t)
                if t > 1:
                    f_copies[s, h, t - 1].wait_recv()
                j = partner(chip, t - 1, chips)
                total = added(total, far(j, weights(s, h, j)))
            if chips > 1:
                f_copies[s, h, chips - 1].wait_recv()
            j = partner(chip, chips - 1, chips)
            total = added(total, far(j, weights(s, h, j)))
            finish(s, h, near_edges(s, h, total))
            if s == 1:
                excess(2, h)

    for copy in sent + list(g_copies.values()) + list(f_copies.values()):
        copy.wait_send()


def hand_out(stress_in, state_in, stress_out, state_out, stress, state, sems):
    moves = [(stress_in, stress, stress_out), (state_in, state, state_out)]
    copies = [pltpu.make_async_copy(a, b, sems.at[0, n]) for n, (a, b, _) in enumerate(moves)]
    for copy in copies:
        copy.start()
    onward = []
    for n, (_, b, c) in enumerate(moves):
        copies[n].wait()
        onward.append(pltpu.make_async_copy(b, c, sems.at[1, n]))
        onward[n].start()
    for copy in onward:
        copy.wait()


def local(stress, state, load_rate, a_param, b_param, near_band, u_far, v_far, ranks):
    rows = lax.axis_size("row")
    cols = lax.axis_size("col")
    members, own = stress.shape
    block_rows, block_cols, slots, dofs = u_far.shape
    chips = rows // 2
    halves = 2 if members % 32 == 0 else 1
    hbm = pl.BlockSpec(memory_space=pltpu.HBM)
    vmem = pl.BlockSpec(memory_space=pltpu.VMEM)
    dma = pltpu.SemaphoreType.DMA
    results = (
        jax.ShapeDtypeStruct(stress.shape, jnp.float32),
        jax.ShapeDtypeStruct(state.shape, jnp.float32),
    )
    stepped = pl.pallas_call(
        functools.partial(kernel, rows, cols),
        out_shape=results,
        in_specs=[hbm] * 9,
        out_specs=(vmem, vmem),
        scratch_shapes=[
            pltpu.VMEM(stress.shape, jnp.float32),
            pltpu.VMEM(state.shape, jnp.float32),
            pltpu.VMEM(load_rate.shape, jnp.int32),
            pltpu.VMEM(a_param.shape, jnp.float32),
            pltpu.VMEM(b_param.shape, jnp.float32),
            pltpu.SMEM(ranks.shape, jnp.int32),
            pltpu.VMEM(near_band.shape, jnp.bfloat16),
            pltpu.VMEM((cols,) + u_far.shape, jnp.bfloat16),
            pltpu.VMEM((cols, dofs, block_rows * block_cols * slots), jnp.bfloat16),
            pltpu.VMEM(v_far.shape, jnp.bfloat16),
            pltpu.VMEM((block_rows, 3, dofs, dofs), jnp.bfloat16),
            pltpu.VMEM((3, halves, rows, members // halves, own), jnp.bfloat16),
            dma((9,)),
            dma((2, cols)),
            dma((2, cols)),
            dma((3, halves, chips)),
            dma((3, halves, chips)),
            dma((3, halves, chips)),
            dma((3, halves, chips)),
        ],
        compiler_params=pltpu.CompilerParams(
            collective_id=0, has_side_effects=True, vmem_limit_bytes=60 * 1024 * 1024
        ),
        cost_estimate=pl.CostEstimate(flops=400_000_000, bytes_accessed=4_000_000, transcendentals=300_000),
    )(stress, state, load_rate, a_param, b_param, near_band, u_far, v_far, ranks)
    anywhere = pl.BlockSpec(memory_space=pl.ANY)
    return pl.pallas_call(
        hand_out,
        out_shape=results,
        in_specs=[anywhere] * 2,
        out_specs=(anywhere, anywhere),
        scratch_shapes=[
            pltpu.VMEM(stress.shape, jnp.float32),
            pltpu.VMEM(state.shape, jnp.float32),
            dma((2, 2)),
        ],
        compiler_params=pltpu.CompilerParams(vmem_limit_bytes=60 * 1024 * 1024),
        cost_estimate=pl.CostEstimate(flops=0, bytes_accessed=400_000, transcendentals=0),
    )(*stepped)


def solution(mesh):
    return jax.shard_map(
        local,
        mesh=mesh,
        in_specs=(
            P("col", "row"),
            P("col", "row"),
            P("col", "row"),
            P("row"),
            P("row"),
            P("row", None),
            P("row", "col", None, None),
            P("row", "col", None, None),
            P("row", "col"),
        ),
        out_specs=(P("col", "row"), P("col", "row")),
        check_vma=False,
    )
```

```python
import functools

import jax
import jax.numpy as jnp
from jax import lax
from jax.experimental import pallas as pl
from jax.experimental.pallas import tpu as pltpu
from jax.sharding import PartitionSpec as P

B = 128
HSTEP = 0.2
RATE_UNIT = 1.0 / 1024.0
MESH = pl.DeviceIdType.MESH


def partner(index, step, count):
    assert count & (count - 1) == 0
    bit = 1
    while bit <= step:
        if step & bit:
            index = index + bit - 2 * bit * ((index // bit) % 2)
        bit *= 2
    return index


def kernel(
    rows,
    cols,
    stress_in,
    state_in,
    load_in,
    a_hbm,
    b_hbm,
    band_in,
    u_in,
    v_in,
    ranks_hbm,
    stress_out,
    state_out,
    stress0,
    state0,
    load,
    a_in,
    b_in,
    ranks,
    band,
    u_all,
    v_all,
    v_own,
    band_t,
    grid,
    load_sem,
    w_send,
    w_recv,
    g_send,
    g_recv,
    f_send,
    f_recv,
):
    row = lax.axis_index("row")
    col = lax.axis_index("col")
    chips = rows // 2
    chip = row // 2
    core = row % 2
    peer = 2 * chip + 1 - core
    _, block_rows, block_cols, slots, dofs = u_all.shape
    _, halves, _, half, _ = grid.shape

    barrier = pltpu.get_barrier_semaphore()
    others = [(row, partner(col, t, cols)) for t in ([1, 2] if cols == 4 else range(1, cols))]
    others += [(2 * partner(chip, t, chips) + core, col) for t in range(1, chips)]
    others += [(peer, col)]
    for other in others:
        pl.semaphore_signal(barrier, inc=1, device_id=other, device_id_type=MESH)

    loads = [
        pltpu.make_async_copy(source, target, load_sem.at[n])
        for n, (source, target) in enumerate(
            [
                (ranks_hbm, ranks),
                (v_in, v_own),
                (u_in, u_all.at[col]),
                (stress_in, stress0),
                (state_in, state0),
                (a_hbm, a_in),
                (b_hbm, b_in),
                (load_in, load),
                (band_in, band),
            ]
        )
    ]
    for copy in loads:
        copy.start()

    loads[1].wait()
    v_all[col] = v_own[...].reshape(block_rows * block_cols * slots, dofs).T

    pl.semaphore_wait(barrier, len(others))

    def send(source, target, send_sem, recv_sem, device):
        copy = pltpu.make_async_remote_copy(
            src_ref=source,
            dst_ref=target,
            send_sem=send_sem,
            recv_sem=recv_sem,
            device_id=device,
            device_id_type=MESH,
        )
        copy.start()
        return copy

    sent = []
    relayed = cols == 4
    col_steps = [1, 2] if relayed else list(range(1, cols))

    def send_factors(kind, source, owner, t, to):
        target = (v_all, u_all)[kind].at[owner]
        copy = send(source, target, w_send.at[kind, t], w_recv.at[kind, t], (row, partner(col, to, cols)))
        sent.append(copy)
        return copy

    v_copies = {}
    u_copies = {}

    def send_first():
        for t in [1] if relayed else col_steps:
            v_copies[t] = send_factors(0, v_all.at[col], col, t, t)
        if relayed:
            u_copies[2] = send_factors(1, u_all.at[col], col, 2, 2)

    def send_second():
        if relayed:
            v_copies[2] = send_factors(0, v_all.at[col], col, 2, 2)
        for t in [1] if relayed else col_steps:
            u_copies[t] = send_factors(1, u_all.at[col], col, t, t)

    def relay_v():
        if relayed:
            v_copies[1].wait_recv()
            owner = partner(col, 1, cols)
            v_copies[3] = send_factors(0, v_all.at[owner], owner, 3, 2)

    def relay_u():
        if relayed:
            u_copies[2].wait_recv()
            owner = partner(col, 2, cols)
            u_copies[3] = send_factors(1, u_all.at[owner], owner, 3, 1)

    def wait_factors(copies, t):
        if not (relayed and t == (1 if copies is v_copies else 2)):
            copies[t].wait_recv()

    def mask_u():
        loads[0].wait()
        loads[2].wait()
        slot = lax.broadcasted_iota(jnp.int32, (slots, dofs), 0)
        for i in range(block_rows):
            for j in range(block_cols):
                spacing = jnp.abs(row * block_rows + i - col * block_cols - j)
                limit = jnp.where(spacing >= 2, ranks[i, j], 0)
                factors = u_all[col, i, j].astype(jnp.float32)
                u_all[col, i, j] = jnp.where(slot < limit, factors, 0.0).astype(jnp.bfloat16)

    def weights(s, h, j):
        per_row = block_cols // 2
        blocks = [
            grid[s, h, 2 * j + n // per_row, :, (n % per_row) * dofs : (n % per_row + 1) * dofs]
            for n in range(block_cols)
        ]
        products = jnp.dot(
            jnp.concatenate(blocks, axis=0), v_all[j], preferred_element_type=jnp.float32
        )
        lane = lax.broadcasted_iota(jnp.int32, (half, block_rows * block_cols * slots), 1)
        owner = (lane // slots) % block_cols
        weight = products[:half]
        for n in range(1, block_cols):
            weight = jnp.where(owner == n, products[n * half : (n + 1) * half], weight)
        return weight.astype(jnp.bfloat16)

    def far(j, weight):
        width = block_cols * slots
        return [
            jnp.dot(
                weight[:, i * width : (i + 1) * width],
                u_all[j, i].reshape(width, dofs),
                preferred_element_type=jnp.float32,
            )
            for i in range(block_rows)
        ]

    def added(total, terms):
        return [old + term for old, term in zip(total, terms)]

    def near_own(s, h):
        total = [None] * block_rows
        for i in range(block_rows):
            for n in range(max(i - 1, 0), min(i + 2, block_rows)):
                term = jnp.dot(
                    grid[s, h, row, :, n * dofs : (n + 1) * dofs],
                    band_t[i, n - i + 1],
                    preferred_element_type=jnp.float32,
                )
                total[i] = term if total[i] is None else total[i] + term
        return total

    def near_edges(s, h, total):
        left = grid[s, h, (row + rows - 1) % rows, :, (block_rows - 1) * dofs :]
        right = grid[s, h, (row + 1) % rows, :, :dofs]
        left_term = jnp.dot(left, band_t[0, 0], preferred_element_type=jnp.float32)
        right_term = jnp.dot(right, band_t[block_rows - 1, 2], preferred_element_type=jnp.float32)
        total = list(total)
        total[0] = total[0] + jnp.where(row > 0, left_term, 0.0)
        total[-1] = total[-1] + jnp.where(row < rows - 1, right_term, 0.0)
        return total

    g_copies = {}
    f_copies = {}

    def stepped(s, start, now, rate):
        if s == 0:
            return start + HSTEP * rate
        if s == 1:
            return 0.75 * start + 0.25 * (now + HSTEP * rate)
        return start / 3.0 + 2.0 / 3.0 * (now + HSTEP * rate)

    def excess(s, h):
        members_now = slice(h * half, (h + 1) * half)
        stress_now, state_now = (stress0, state0) if s == 0 else (stress_out, state_out)
        later = []
        for i in range(block_rows):
            lanes = slice(i * B, (i + 1) * B)
            theta = state_now[members_now, lanes]
            direct = a_in[lanes].reshape(1, B)
            squares = None
            for d in range(2):
                dof = slice((2 * i + d) * B, (2 * i + d + 1) * B)
                scaled = stress_now[members_now, dof] / direct
                rate = jnp.exp(scaled - theta) - jnp.exp(-scaled - theta)
                plate = load[members_now, dof].astype(jnp.float32) * RATE_UNIT
                grid[s, h, row, :, dof] = (rate - plate).astype(jnp.bfloat16)
                squares = rate * rate if squares is None else squares + rate * rate
            later.append((lanes, theta, squares))
        mine = grid.at[s, h, row]
        f_copies[s, h, 0] = send(mine, mine, f_send.at[s, h, 0], f_recv.at[s, h, 0], (peer, col))
        for t in list(range(2, chips)) + list(range(1, min(2, chips))):
            g_copies[s, h, t] = send(
                mine,
                mine,
                g_send.at[s, h, t],
                g_recv.at[s, h, t],
                (2 * partner(chip, t, chips) + core, col),
            )
        for lanes, theta, squares in later:
            drift = b_in[lanes].reshape(1, B) * (jnp.exp(-theta) - jnp.sqrt(squares))
            state_out[members_now, lanes] = stepped(s, state0[members_now, lanes], theta, drift)

    def relay(s, h, t):
        g_copies[s, h, t].wait_recv()
        got = grid.at[s, h, 2 * partner(chip, t, chips) + core]
        f_copies[s, h, t] = send(got, got, f_send.at[s, h, t], f_recv.at[s, h, t], (peer, col))

    def finish(s, h, total):
        members_now = slice(h * half, (h + 1) * half)
        stress_now = stress0 if s == 0 else stress_out
        for i in range(block_rows):
            lanes = slice(i * dofs, (i + 1) * dofs)
            stress_out[members_now, lanes] = stepped(
                s, stress0[members_now, lanes], stress_now[members_now, lanes], -total[i]
            )

    mask_u()
    send_first()
    for copy in loads[3:8]:
        copy.wait()
    for h in range(halves):
        excess(0, h)
    send_second()
    relay_v()
    relay_u()
    loads[8].wait()
    for i in range(block_rows):
        for n in range(3):
            band_t[i, n] = band[i * dofs : (i + 1) * dofs, n * dofs : (n + 1) * dofs].T
    for h in range(halves):
        for t in range(1, chips):
            relay(0, h, t)
    totals = [near_own(0, h) for h in range(halves)]
    for h in range(halves):
        for t in range(chips):
            f_copies[0, h, t].wait_recv()
        totals[h] = near_edges(0, h, totals[h])
    ready = []
    for t in range(cols):
        j = partner(col, t, cols)
        if t > 0:
            wait_factors(v_copies, t)
        ready.append((j, [weights(0, h, j) for h in range(halves)]))
    for t, (j, weight) in enumerate(ready):
        if t > 0:
            wait_factors(u_copies, t)
        for h in range(halves):
            totals[h] = added(totals[h], far(j, weight[h]))
            if t == cols - 1:
                finish(0, h, totals[h])
                excess(1, h)

    for s in (1, 2):
        for h in range(halves):
            total = near_own(s, h)
            f_copies[s, h, 0].wait_recv()
            for t in range(1, chips):
                if (s, h, t) not in f_copies:
                    relay(s, h, t)
                if t > 1:
                    f_copies[s, h, t - 1].wait_recv()
                j = partner(chip, t - 1, chips)
                total = added(total, far(j, weights(s, h, j)))
            if h + 1 < halves:
                for t in range(1, chips - 1):
                    relay(s, h + 1, t)
            if chips > 1:
                f_copies[s, h, chips - 1].wait_recv()
            j = partner(chip, chips - 1, chips)
            total = added(total, far(j, weights(s, h, j)))
            finish(s, h, near_edges(s, h, total))
            if s == 1:
                excess(2, h)

    for copy in sent + list(g_copies.values()) + list(f_copies.values()):
        copy.wait_send()


def hand_out(stress_in, state_in, stress_out, state_out, stress, state, sems):
    moves = [(stress_in, stress, stress_out), (state_in, state, state_out)]
    copies = [pltpu.make_async_copy(a, b, sems.at[0, n]) for n, (a, b, _) in enumerate(moves)]
    for copy in copies:
        copy.start()
    onward = []
    for n, (_, b, c) in enumerate(moves):
        copies[n].wait()
        onward.append(pltpu.make_async_copy(b, c, sems.at[1, n]))
        onward[n].start()
    for copy in onward:
        copy.wait()


def local(stress, state, load_rate, a_param, b_param, near_band, u_far, v_far, ranks):
    rows = lax.axis_size("row")
    cols = lax.axis_size("col")
    members, own = stress.shape
    block_rows, block_cols, slots, dofs = u_far.shape
    chips = rows // 2
    halves = 2 if members % 32 == 0 else 1
    hbm = pl.BlockSpec(memory_space=pltpu.HBM)
    vmem = pl.BlockSpec(memory_space=pltpu.VMEM)
    dma = pltpu.SemaphoreType.DMA
    results = (
        jax.ShapeDtypeStruct(stress.shape, jnp.float32),
        jax.ShapeDtypeStruct(state.shape, jnp.float32),
    )
    stepped = pl.pallas_call(
        functools.partial(kernel, rows, cols),
        out_shape=results,
        in_specs=[hbm] * 9,
        out_specs=(vmem, vmem),
        scratch_shapes=[
            pltpu.VMEM(stress.shape, jnp.float32),
            pltpu.VMEM(state.shape, jnp.float32),
            pltpu.VMEM(load_rate.shape, jnp.int32),
            pltpu.VMEM(a_param.shape, jnp.float32),
            pltpu.VMEM(b_param.shape, jnp.float32),
            pltpu.SMEM(ranks.shape, jnp.int32),
            pltpu.VMEM(near_band.shape, jnp.bfloat16),
            pltpu.VMEM((cols,) + u_far.shape, jnp.bfloat16),
            pltpu.VMEM((cols, dofs, block_rows * block_cols * slots), jnp.bfloat16),
            pltpu.VMEM(v_far.shape, jnp.bfloat16),
            pltpu.VMEM((block_rows, 3, dofs, dofs), jnp.bfloat16),
            pltpu.VMEM((3, halves, rows, members // halves, own), jnp.bfloat16),
            dma((9,)),
            dma((2, cols)),
            dma((2, cols)),
            dma((3, halves, chips)),
            dma((3, halves, chips)),
            dma((3, halves, chips)),
            dma((3, halves, chips)),
        ],
        compiler_params=pltpu.CompilerParams(
            collective_id=0, has_side_effects=True, vmem_limit_bytes=60 * 1024 * 1024
        ),
        cost_estimate=pl.CostEstimate(flops=400_000_000, bytes_accessed=4_000_000, transcendentals=300_000),
    )(stress, state, load_rate, a_param, b_param, near_band, u_far, v_far, ranks)
    anywhere = pl.BlockSpec(memory_space=pl.ANY)
    return pl.pallas_call(
        hand_out,
        out_shape=results,
        in_specs=[anywhere] * 2,
        out_specs=(anywhere, anywhere),
        scratch_shapes=[
            pltpu.VMEM(stress.shape, jnp.float32),
            pltpu.VMEM(state.shape, jnp.float32),
            dma((2, 2)),
        ],
        compiler_params=pltpu.CompilerParams(vmem_limit_bytes=60 * 1024 * 1024),
        cost_estimate=pl.CostEstimate(flops=0, bytes_accessed=400_000, transcendentals=0),
    )(*stepped)


def solution(mesh):
    return jax.shard_map(
        local,
        mesh=mesh,
        in_specs=(
            P("col", "row"),
            P("col", "row"),
            P("col", "row"),
            P("row"),
            P("row"),
            P("row", None),
            P("row", "col", None, None),
            P("row", "col", None, None),
            P("row", "col"),
        ),
        out_specs=(P("col", "row"), P("col", "row")),
        check_vma=False,
    )
```
